512 devices in a mesh: gx: 8 (over x, y_lo), gy: 8 (over z), gz: 8 (over y_hi, core).
Axes of the slice: x: 4, y: 8 (y_hi: 4, y_lo: 2; y = y_hi * 2 + y_lo), z: 8, core: 2. Of those that a mesh axis runs over, the one named last changes fastest.
Arguments:
- tokens: bfloat16 [2048, 7168], P(('gy', 'gx'), 'gz'), may hold values from -6 to 6
- w_up: bfloat16 [7168, 28672], P('gz', ('gx', 'gy')), may hold values from -0.1875 to 0.1875
- act_grad: bfloat16 [2048, 28672], P('gy', ('gx', 'gz')), may hold values from -6 to 6
Outputs:
- activated: bfloat16 [2048, 28672], P('gy', ('gx', 'gz'))
- input_grad: bfloat16 [2048, 7168], P(('gy', 'gx'), 'gz')
- weight_grad: bfloat16 [7168, 28672], P('gz', ('gx', 'gy'))
The draws below stay inside these ranges and needn't reach their ends.
All inputs are finite; a program needn't handle non-finite values.
Results may differ from the reference program's by a relative error of at most 0.022.
Values may be sent and summed in bfloat16 or wider, within the bound.
No kernel may reach another device: no remote copies, remote signals or barrier semaphores. Data moves between devices by JAX's collectives and lax.ppermute only.
A program may use at most 64 MiB of HBM per device.

```python
import jax
import jax.numpy as jnp
from jax import lax

D = 7168
FF = 28672
TOKENS = 2048
N_GX = 8
N_GZ = 8


def spiked(values, rng, source, target, parts, factor):
    owner, partner = [(jnp.arange(values.shape[axis_at]) // (values.shape[axis_at] // parts)).reshape([-1 if axis == axis_at else 1 for axis in range(values.ndim)]) for axis_at in (source, target)]
    chosen = jax.random.permutation(rng, parts)[partner]
    strong = (owner == chosen) | (owner == (partner + parts // 2) % parts)
    return jnp.where(strong, factor * values, values)


def block_scale(stream_key, dims, cuts, low, top_value):
    def one(dim, shards_of):
        heights = jax.random.uniform(jax.random.fold_in(jax.random.fold_in(stream_key, 6), dim), (shards_of,), jnp.float32, low / len(cuts), top_value / len(cuts))
        return jnp.repeat(jnp.exp(heights), dims[dim] // shards_of).reshape((-1,) + (1,) * (len(dims) - dim - 1))

    loudness = one(*cuts[0])
    for cut in cuts[1:]:
        loudness = loudness * one(*cut)
    return loudness


def noise(stream_key, extent, deviation, reach, cuts=(), held_as=jnp.bfloat16):
    array = deviation * jax.random.normal(stream_key, extent, jnp.float32)
    if cuts:
        array = array * block_scale(stream_key, extent, cuts, -0.22, 0.18)
    return jnp.clip(array, -reach, reach).astype(held_as)


def noise_with(key, shape, deviation, limit, pieces, heavy, kind=jnp.bfloat16):
    array = deviation * jax.random.normal(key, shape, jnp.float32)
    if pieces:
        array = array * block_scale(key, shape, pieces, -0.22, 0.18)
    return jnp.clip(spiked(array, jax.random.fold_in(key, 3), *heavy), -limit, limit).astype(kind)


def setup_inputs(seed: int = 0) -> dict:
    keys = jax.random.split(jax.random.key(seed), 4)
    return {
        "tokens": noise(keys[0], (TOKENS, D), 1.0, 6.0, ((0, 64), (1, 8))),
        "w_up": noise_with(keys[1], (D, FF), D ** -0.5, 0.1875, ((0, 8), (1, 64)), (0, 1, 64, 4.0)),
        "act_grad": noise(keys[2], (TOKENS, FF), 1.0, 6.0, ((0, 8), (1, 64))),
    }


def gelu_tanh(values):
    return jax.nn.gelu(values, approximate=True)

def reference(tokens, w_up, act_grad):
    feat_block = D // N_GZ
    hidden = jnp.zeros((TOKENS, FF), jnp.float32)
    for piece_index in range(N_GZ):
        lower = piece_index * feat_block
        partial_value = jnp.dot(tokens[:, lower:lower + feat_block], w_up[lower:lower + feat_block], preferred_element_type=jnp.float32).astype(jnp.bfloat16)
        hidden = hidden + lax.optimization_barrier(partial_value).astype(jnp.float32)
    activated, pullback = jax.vjp(gelu_tanh, hidden)
    hidden_grad = pullback(act_grad.astype(jnp.float32))[0].astype(jnp.bfloat16)
    activated = activated.astype(jnp.bfloat16)
    weight_grad = lax.dot_general(tokens, hidden_grad, (((0,), (0,)), ((), ())), preferred_element_type=jnp.float32).astype(jnp.bfloat16)
    unit_block = FF // N_GX
    total = jnp.zeros((TOKENS, D), jnp.float32)
    for piece_index in range(N_GX):
        lower = piece_index * unit_block
        partial_value = lax.dot_general(hidden_grad[:, lower:lower + unit_block], w_up[:, lower:lower + unit_block], (((1,), (1,)), ((), ())), preferred_element_type=jnp.float32).astype(jnp.bfloat16)
        total = total + lax.optimization_barrier(partial_value).astype(jnp.float32)
    input_grad = total.astype(jnp.bfloat16)
    return (activated, input_grad, weight_grad)
```

```python
import jax
import jax.numpy as jnp
from jax import lax
from jax.sharding import Mesh
from jax.sharding import PartitionSpec as P

AXES = ("x", "yl", "z", "yh", "c")
NX = 4
BF = jnp.bfloat16


def gelu_tanh(values):
    return jax.nn.gelu(values, approximate=True)


def along_x(value, shift):
    return lax.ppermute(value, "x", [(i, (i + shift) % NX) for i in range(NX)])


def swap_cores(value):
    return lax.ppermute(value, "c", [(0, 1), (1, 0)])


def swap_z_g(value):
    pairs = [(a * 8 + b, b * 8 + a) for a in range(8) for b in range(8)]
    return lax.ppermute(value, ("z", "yh", "c"), pairs)


def dot_nt(a, b):
    return lax.dot_general(a, b, (((1,), (1,)), ((), ())), preferred_element_type=jnp.float32)


def dot_nn(a, b):
    return lax.dot_general(a, b, (((1,), (0,)), ((), ())), preferred_element_type=jnp.float32)


def dot_tn(a, b):
    return lax.dot_general(a, b, (((0,), (0,)), ((), ())), preferred_element_type=jnp.float32)


def body(tokens, w_up, act_grad):
    rows, feats = tokens.shape
    cols = w_up.shape[1]
    pair = 2 * rows
    core = lax.axis_index("c")
    here = lax.axis_index("x")

    w_own = w_up.T
    w_low = along_x(w_own, 1)
    w_high = along_x(w_own, -1)
    half = cols // 2
    w_far = jnp.concatenate([along_x(w_high[:half], -1), along_x(w_low[half:], 1)], axis=0)
    w_all = jnp.concatenate([w_own, w_high, w_far, w_low], axis=0)

    near = lax.all_gather(tokens, "yl", axis=0, tiled=True)
    near = lax.all_gather(near, "z", axis=0, tiled=False).reshape(4, 2, pair, feats)
    mine = lax.dynamic_index_in_dim(near, core, 1, keepdims=False).reshape(4 * pair, feats)
    theirs = lax.dynamic_index_in_dim(near, 1 - core, 1, keepdims=False).reshape(4 * pair, feats)

    cot = swap_z_g(act_grad)
    cot = lax.all_to_all(cot.reshape(NX, pair, cols), "x", split_axis=0, concat_axis=0)
    order = (here + jnp.arange(NX)) % NX
    cot = jnp.take(cot, order, axis=0)

    sent = swap_cores(dot_nt(theirs, w_all).astype(BF))
    partial_value = (dot_nt(mine, w_all) + sent.astype(jnp.float32)).astype(BF)
    partial_value = partial_value.reshape(4, pair, NX * cols)
    parts = lax.all_to_all(partial_value, "yh", split_axis=0, concat_axis=0)
    hidden = jnp.sum(parts.astype(jnp.float32), axis=0)
    hidden = hidden.reshape(pair, NX, cols).transpose(1, 0, 2)

    activated, pullback = jax.vjp(gelu_tanh, hidden)
    hidden_grad = pullback(cot.astype(jnp.float32))[0].astype(BF)
    activated = activated.astype(BF)

    grad_half = lax.all_gather(
        hidden_grad.transpose(1, 0, 2).reshape(pair, NX * cols), "yh", axis=0, tiled=True
    )
    grad_other = swap_cores(grad_half)
    blocks = [grad_half[:, r * cols : (r + 1) * cols] for r in range(NX)]
    blocks = [blocks[0]] + [along_x(blocks[r], r) for r in range(1, NX)]
    order = (here - jnp.arange(NX)) % NX
    cols_mine = jnp.concatenate(blocks, axis=0)
    cols_theirs = swap_cores(cols_mine)

    ig_mine = dot_nn(grad_half, w_all).astype(BF).reshape(4, pair, feats)
    ig_theirs = dot_nn(grad_other, w_all).astype(BF).reshape(4, pair, feats)
    first = jnp.where(core == 0, ig_mine, ig_theirs)
    second = jnp.where(core == 0, ig_theirs, ig_mine)
    ig = jnp.stack([first, second], axis=1).reshape(16, rows, feats)
    ig = lax.all_to_all(ig, ("z", "yl"), split_axis=0, concat_axis=0)
    input_grad = jnp.sum(ig.astype(jnp.float32), axis=0).astype(BF)

    far = lax.all_gather(jnp.stack([mine, theirs]), "x", axis=0, tiled=False)
    far = jnp.take(far, order, axis=0)
    weight_grad = dot_tn(far[:, 0].reshape(-1, feats), cols_mine)
    weight_grad = weight_grad + dot_tn(far[:, 1].reshape(-1, feats), cols_theirs)
    weight_grad = weight_grad.astype(BF)

    order = (jnp.arange(NX) - here) % NX
    out = jnp.take(activated, order, axis=0)
    out = lax.all_to_all(out, "x", split_axis=0, concat_axis=0).reshape(NX * pair, cols)
    out = swap_z_g(out)
    return out, input_grad, weight_grad


def solution(mesh):
    fine = Mesh(mesh.devices.reshape(NX, 2, 8, 4, 2), AXES)
    in_specs = (P(("z", "x", "yl"), ("yh", "c")), P(("yh", "c"), ("x", "yl", "z")), P("z", ("x", "yl", "yh", "c")))
    out_specs = (in_specs[2], in_specs[0], in_specs[1])
    return jax.shard_map(body, mesh=fine, in_specs=in_specs, out_specs=out_specs, check_vma=False)
```

```python
import jax
import jax.numpy as jnp
from jax import lax
from jax.sharding import Mesh
from jax.sharding import PartitionSpec as P

AXES = ("x", "yl", "z", "yh", "c")
NX = 4
BF = jnp.bfloat16


def gelu_tanh(values):
    return jax.nn.gelu(values, approximate=True)


def along_x(value, shift):
    return lax.ppermute(value, "x", [(i, (i + shift) % NX) for i in range(NX)])


def swap_cores(value):
    return lax.ppermute(value, "c", [(0, 1), (1, 0)])


def swap_z_g(value, shift):
    pairs = []
    for x in range(NX):
        for a in range(8):
            for b in range(8):
                pairs.append((x * 64 + a * 8 + b, (x + shift) % NX * 64 + b * 8 + a))
    return lax.ppermute(value, ("x", "z", "yh", "c"), pairs)


def pick(blocks, index):
    return lax.dynamic_index_in_dim(blocks, index & (NX - 1), 0, keepdims=False)


def dot_nt(a, b):
    return lax.dot_general(a, b, (((1,), (1,)), ((), ())), preferred_element_type=jnp.float32)


def dot_nn(a, b):
    return lax.dot_general(a, b, (((1,), (0,)), ((), ())), preferred_element_type=jnp.float32)


def dot_tn(a, b):
    return lax.dot_general(a, b, (((0,), (0,)), ((), ())), preferred_element_type=jnp.float32)


def body(tokens, w_up, act_grad):
    rows, feats = tokens.shape
    cols = w_up.shape[1]
    pair = 2 * rows
    core = lax.axis_index("c").astype(jnp.uint32)
    here = lax.axis_index("x").astype(jnp.uint32)

    w_own = w_up.T
    w_low = along_x(w_own, 1)
    w_high = along_x(w_own, -1)
    half = cols // 2
    far_top = along_x(w_high[:half], -1)
    far_bottom = along_x(w_low[half:], 1)

    cot = act_grad.reshape(NX, pair, cols)
    cot = [swap_z_g(pick(cot, here + (NX - r)), -r) for r in range(NX)]

    near = jnp.broadcast_to(tokens[None], (16, rows, feats))
    near = lax.all_to_all(near, ("z", "yl"), split_axis=0, concat_axis=0)
    near, *cot = lax.optimization_barrier((near, *cot))
    near = near.reshape(4, 2, pair, feats)
    mine = lax.dynamic_index_in_dim(near, core, 1, keepdims=False).reshape(4 * pair, feats)
    theirs = lax.dynamic_index_in_dim(near, core ^ 1, 1, keepdims=False).reshape(4 * pair, feats)

    w_all = jnp.concatenate([w_own, w_high, far_top, far_bottom, w_low], axis=0)
    sent = swap_cores(dot_nt(theirs, w_all).astype(BF))
    partial_value = (dot_nt(mine, w_all) + sent.astype(jnp.float32)).astype(BF)
    partial_value = partial_value.reshape(4, pair, NX * cols)
    parts = lax.all_to_all(partial_value, "yh", split_axis=0, concat_axis=0)
    hidden = jnp.sum(parts.astype(jnp.float32), axis=0)

    activated, pullback = jax.vjp(gelu_tanh, hidden)
    hidden_grad = pullback(jnp.concatenate(cot, axis=1).astype(jnp.float32))[0].astype(BF)
    activated = activated.astype(BF)

    grad_half = lax.all_gather(hidden_grad, "yh", axis=0, tiled=True)
    grad_other = swap_cores(grad_half)
    ig_mine = dot_nn(grad_half, w_all).astype(BF).reshape(4, pair, feats)
    ig_theirs = dot_nn(grad_other, w_all).astype(BF).reshape(4, pair, feats)
    first = jnp.where(core == 0, ig_mine, ig_theirs)
    second = jnp.where(core == 0, ig_theirs, ig_mine)
    ig = jnp.stack([first, second], axis=1).reshape(16, rows, feats)
    ig, grad_half, activated = lax.optimization_barrier((ig, grad_half, activated))
    ig = lax.all_to_all(ig, ("z", "yl"), split_axis=0, concat_axis=0)
    input_grad = jnp.sum(ig.astype(jnp.float32), axis=0).astype(BF)

    cols_mine = jnp.zeros((NX, 4 * pair, cols), BF)
    for r in range(NX):
        block = grad_half[:, r * cols : (r + 1) * cols]
        block = along_x(block, r) if r else block
        cols_mine = lax.dynamic_update_index_in_dim(cols_mine, block, (here + (NX - r)) & (NX - 1), 0)
    cols_theirs = swap_cores(cols_mine)
    far_cols = jnp.stack([cols_mine, cols_theirs], axis=1).reshape(-1, cols)
    far = lax.all_gather(jnp.stack([mine, theirs]), "x", axis=0, tiled=False)
    weight_grad = dot_tn(far.reshape(-1, feats), far_cols).astype(BF)

    out = jnp.zeros((NX, pair, cols), BF)
    for r in range(NX):
        block = swap_z_g(activated[:, r * cols : (r + 1) * cols], r)
        out = lax.dynamic_update_index_in_dim(out, block, (here + (NX - r)) & (NX - 1), 0)
    return out.reshape(NX * pair, cols), input_grad, weight_grad


def solution(mesh):
    fine = Mesh(mesh.devices.reshape(NX, 2, 8, 4, 2), AXES)
    in_specs = (P(("z", "x", "yl"), ("yh", "c")), P(("yh", "c"), ("x", "yl", "z")), P("z", ("x", "yl", "yh", "c")))
    out_specs = (in_specs[2], in_specs[0], in_specs[1])
    return jax.shard_map(body, mesh=fine, in_specs=in_specs, out_specs=out_specs, check_vma=False)
```

```python
import jax
import jax.numpy as jnp
from jax import lax
from jax.sharding import Mesh
from jax.sharding import PartitionSpec as P

AXES = ("x", "yl", "z", "yh", "c")
NX = 4
BF = jnp.bfloat16


def gelu_tanh(values):
    return jax.nn.gelu(values, approximate=True)


def along_x(value, shift):
    return lax.ppermute(value, "x", [(i, (i + shift) % NX) for i in range(NX)])


def swap_cores(value):
    return lax.ppermute(value, "c", [(0, 1), (1, 0)])


def swap_z_g(value):
    pairs = [(a * 8 + b, b * 8 + a) for a in range(8) for b in range(8)]
    return lax.ppermute(value, ("z", "yh", "c"), pairs)


def pick(blocks, index):
    return lax.dynamic_index_in_dim(blocks, index & (NX - 1), 0, keepdims=False)


def dot_nt(a, b):
    return lax.dot_general(a, b, (((1,), (1,)), ((), ())), preferred_element_type=jnp.float32)


def dot_nn(a, b):
    return lax.dot_general(a, b, (((1,), (0,)), ((), ())), preferred_element_type=jnp.float32)


def dot_tn(a, b):
    return lax.dot_general(a, b, (((0,), (0,)), ((), ())), preferred_element_type=jnp.float32)


def body(tokens, w_up, act_grad):
    rows, feats = tokens.shape
    cols = w_up.shape[1]
    pair = 2 * rows
    core = lax.axis_index("c").astype(jnp.uint32)
    here = lax.axis_index("x").astype(jnp.uint32)

    w_own = w_up.T
    w_low = along_x(w_own, 1)
    w_high = along_x(w_own, -1)
    half = cols // 2
    cot = swap_z_g(act_grad)
    far_top = along_x(w_high[:half], -1)
    far_bottom = along_x(w_low[half:], 1)


    near = jnp.broadcast_to(tokens[None], (16, rows, feats))
    near = lax.all_to_all(near, ("z", "yl"), split_axis=0, concat_axis=0)
    near, cot = lax.optimization_barrier((near, cot))
    near = near.reshape(4, 2, pair, feats)
    mine = lax.dynamic_index_in_dim(near, core, 1, keepdims=False).reshape(4 * pair, feats)
    theirs = lax.dynamic_index_in_dim(near, core ^ 1, 1, keepdims=False).reshape(4 * pair, feats)

    w_all = jnp.concatenate([w_own, w_high, far_top, far_bottom, w_low], axis=0)
    sent = swap_cores(dot_nt(theirs, w_all).astype(BF))
    partial_value = (dot_nt(mine, w_all) + sent.astype(jnp.float32)).astype(BF)
    partial_value, cot = lax.optimization_barrier((partial_value, cot))
    cot = cot.reshape(NX, pair, cols)
    cot = [pick(cot, here + (NX - r)) for r in range(NX)]
    cot = [along_x(cot[r], -r) if r else cot[r] for r in range(NX)]
    cot = jnp.concatenate(cot, axis=1)
    partial_value = partial_value.reshape(4, pair, NX * cols)
    parts = lax.all_to_all(partial_value, "yh", split_axis=0, concat_axis=0)
    hidden = jnp.sum(parts.astype(jnp.float32), axis=0)

    activated, pullback = jax.vjp(gelu_tanh, hidden)
    hidden_grad = pullback(cot.astype(jnp.float32))[0].astype(BF)
    activated = activated.astype(BF)

    grad_half = lax.all_gather(hidden_grad, "yh", axis=0, tiled=True)
    grad_half, activated = lax.optimization_barrier((grad_half, activated))
    grad_other = swap_cores(grad_half)
    activated = swap_z_g(activated)
    ig_mine = dot_nn(grad_half, w_all).astype(BF).reshape(4, pair, feats)
    ig_theirs = dot_nn(grad_other, w_all).astype(BF).reshape(4, pair, feats)
    first = jnp.where(core == 0, ig_mine, ig_theirs)
    second = jnp.where(core == 0, ig_theirs, ig_mine)
    ig = jnp.stack([first, second], axis=1).reshape(16, rows, feats)
    ig, grad_half = lax.optimization_barrier((ig, grad_half))
    ig = lax.all_to_all(ig, ("z", "yl"), split_axis=0, concat_axis=0)
    input_grad = jnp.sum(ig.astype(jnp.float32), axis=0).astype(BF)

    cols_mine = jnp.zeros((NX, 4 * pair, cols), BF)
    for r in range(NX):
        block = grad_half[:, r * cols : (r + 1) * cols]
        block = along_x(block, r) if r else block
        cols_mine = lax.dynamic_update_index_in_dim(cols_mine, block, (here + (NX - r)) & (NX - 1), 0)
    cols_theirs = swap_cores(cols_mine)
    far_cols = jnp.stack([cols_mine, cols_theirs], axis=1).reshape(-1, cols)
    far = lax.all_gather(jnp.stack([mine, theirs]), "x", axis=0, tiled=False)
    weight_grad = dot_tn(far.reshape(-1, feats), far_cols).astype(BF)

    out = jnp.zeros((NX, pair, cols), BF)
    for r in range(NX):
        block = activated[:, r * cols : (r + 1) * cols]
        block = along_x(block, r) if r else block
        out = lax.dynamic_update_index_in_dim(out, block, (here + (NX - r)) & (NX - 1), 0)
    return out.reshape(NX * pair, cols), input_grad, weight_grad


def solution(mesh):
    fine = Mesh(mesh.devices.reshape(NX, 2, 8, 4, 2), AXES)
    in_specs = (P(("z", "x", "yl"), ("yh", "c")), P(("yh", "c"), ("x", "yl", "z")), P("z", ("x", "yl", "yh", "c")))
    out_specs = (in_specs[2], in_specs[0], in_specs[1])
    return jax.shard_map(body, mesh=fine, in_specs=in_specs, out_specs=out_specs, check_vma=False)
```

```python
import jax
import jax.numpy as jnp
from jax import lax
from jax.sharding import Mesh
from jax.sharding import PartitionSpec as P

AXES = ("x", "yl", "z", "yh", "c")
NX = 4
BF = jnp.bfloat16
GROUPS = [
    [(2 * h + (c ^ p)) * 4 + l * 2 + c for p in range(2) for h in range(4) for l in range(2)] for c in range(2)
]


def gelu_tanh(values):
    return jax.nn.gelu(values, approximate=True)


def along_x(value, shift):
    return lax.ppermute(value, "x", [(i, (i + shift) % NX) for i in range(NX)])


def swap_cores(value):
    return lax.ppermute(value, "c", [(0, 1), (1, 0)])


def homes():
    for x in range(NX):
        for zh in range(4):
            for zc in range(2):
                for g in range(8):
                    yield x * 64 + (zh * 2 + zc) * 8 + g, zh * 64 + g * 8 + x * 2 + zc


def from_home(value):
    return lax.ppermute(value, ("x", "z", "yh", "c"), [(a, b) for a, b in homes()])


def to_home(value):
    return lax.ppermute(value, ("x", "z", "yh", "c"), [(b, a) for a, b in homes()])


def exchange_rows(value):
    return lax.all_to_all(
        value, ("z", "yl", "c"), split_axis=0, concat_axis=0, axis_index_groups=GROUPS
    )


def dot(a, b, contract):
    return lax.dot_general(a, b, (contract, ((), ())), preferred_element_type=jnp.float32)


def body(tokens, w_up, act_grad):
    rows, feats = tokens.shape
    cols = w_up.shape[1]
    pair = 2 * rows
    here = lax.axis_index("x").astype(jnp.uint32)

    w_all = lax.all_gather(w_up.T, "x", axis=0, tiled=False)

    near = exchange_rows(jnp.broadcast_to(tokens[None], (16, rows, feats)))
    near = near.reshape(2, 4 * pair, feats)

    near, cot = lax.optimization_barrier((near, from_home(act_grad)))
    cot = lax.all_to_all(cot.reshape(NX, pair, cols), "x", split_axis=0, concat_axis=0)
    cot = cot.reshape(NX * pair, cols).T
    w_all, near, cot = lax.optimization_barrier((w_all, near, cot))

    sent = swap_cores(dot(w_all, near[1], ((2,), (1,))).astype(BF))
    partial_value = (dot(w_all, near[0], ((2,), (1,))) + sent.astype(jnp.float32)).astype(BF)
    parts = lax.all_to_all(partial_value, "yh", split_axis=0, concat_axis=0)
    hidden = jnp.sum(parts.astype(jnp.float32), axis=0)

    activated, pullback = jax.vjp(gelu_tanh, hidden)
    hidden_grad = pullback(cot.astype(jnp.float32))[0].astype(BF)
    activated = activated.astype(BF)

    grad_own = lax.all_gather(hidden_grad, "yh", axis=0, tiled=False)
    grad_own, activated = lax.optimization_barrier((grad_own, activated))
    grad_other = swap_cores(grad_own)

    pieces = activated.T.reshape(NX, pair, cols)
    blocks = []
    for r in range(NX):
        block = lax.dynamic_index_in_dim(pieces, (here + r) & (NX - 1), 0, keepdims=False)
        blocks.append(along_x(block, r) if r else block)

    ig_own = dot(grad_own, w_all, ((0, 1), (0, 1))).astype(BF)
    ig_own, grad_other, *blocks = lax.optimization_barrier((ig_own, grad_other, *blocks))
    out = jnp.zeros((NX, pair, cols), BF)
    for r in range(NX):
        out = lax.dynamic_update_index_in_dim(out, blocks[r], (here + (NX - r)) & (NX - 1), 0)
    out = out.reshape(NX * pair, cols)
    ig_other = dot(grad_other, w_all, ((0, 1), (0, 1))).astype(BF)
    ig = jnp.stack([ig_own, ig_other]).reshape(16, rows, feats)
    ig, grad_own, out = lax.optimization_barrier((ig, grad_own, out))
    out = to_home(out)
    ig = exchange_rows(ig)
    input_grad = jnp.sum(ig.astype(jnp.float32), axis=0).astype(BF)

    far_own = jnp.zeros((NX, cols, 4 * pair), BF)
    for r in range(NX):
        block = lax.dynamic_index_in_dim(grad_own, (here + r) & (NX - 1), 0, keepdims=False)
        block = along_x(block, r) if r else block
        far_own = lax.dynamic_update_index_in_dim(far_own, block, (here + (NX - r)) & (NX - 1), 0)
    far_other = swap_cores(far_own)
    far = lax.all_gather(near, "x", axis=0, tiled=False)
    far_grad = jnp.stack([far_own, far_other], axis=1)
    far_grad = far_grad.transpose(2, 0, 1, 3).reshape(cols, -1)
    weight_grad = dot(far_grad, far.reshape(-1, feats), ((1,), (0,))).astype(BF).T
    return out, input_grad, weight_grad


def solution(mesh):
    fine = Mesh(mesh.devices.reshape(NX, 2, 8, 4, 2), AXES)
    in_specs = (P(("z", "x", "yl"), ("yh", "c")), P(("yh", "c"), ("x", "yl", "z")), P("z", ("x", "yl", "yh", "c")))
    out_specs = (in_specs[2], in_specs[0], in_specs[1])
    return jax.shard_map(body, mesh=fine, in_specs=in_specs, out_specs=out_specs, check_vma=False)
```

```python
import jax
import jax.numpy as jnp
from jax import lax
from jax.sharding import Mesh
from jax.sharding import PartitionSpec as P

AXES = ("x", "yl", "z", "yh", "c")
NX = 4
BF = jnp.bfloat16
GROUPS = [
    [(2 * h + (c ^ p)) * 4 + l * 2 + c for p in range(2) for h in range(4) for l in range(2)] for c in range(2)
]


def gelu_tanh(values):
    return jax.nn.gelu(values, approximate=True)


def along_x(value, shift):
    return lax.ppermute(value, "x", [(i, (i + shift) % NX) for i in range(NX)])


def swap_cores(value):
    return lax.ppermute(value, "c", [(0, 1), (1, 0)])


def swap_z_g(value):
    pairs = [(a * 8 + b, b * 8 + a) for a in range(8) for b in range(8)]
    return lax.ppermute(value, ("z", "yh", "c"), pairs)


def shift_blocks(blocks, here):
    parts = []
    for r in range(NX):
        block = lax.dynamic_index_in_dim(blocks, (here + r) & (NX - 1), 0, keepdims=False)
        parts.append(along_x(block, r) if r else block)
    return parts


def in_order(parts, here):
    out = jnp.zeros((NX,) + parts[0].shape, BF)
    for r in range(NX):
        out = lax.dynamic_update_index_in_dim(out, parts[r], (here + (NX - r)) & (NX - 1), 0)
    return out


def exchange_rows(value):
    return lax.all_to_all(
        value, ("z", "yl", "c"), split_axis=0, concat_axis=0, axis_index_groups=GROUPS
    )


def dot(a, b, contract):
    return lax.dot_general(a, b, (contract, ((), ())), preferred_element_type=jnp.float32)


def body(tokens, w_up, act_grad):
    rows, feats = tokens.shape
    cols = w_up.shape[1]
    pair = 2 * rows
    here = lax.axis_index("x").astype(jnp.uint32)

    w_all = lax.all_gather(w_up.T, "x", axis=0, tiled=False)

    near = exchange_rows(jnp.broadcast_to(tokens[None], (16, rows, feats)))
    near = near.reshape(2, 4 * pair, feats)

    near, cot, w_all = lax.optimization_barrier((near, swap_z_g(act_grad), w_all))
    w_all = w_all.reshape(NX * cols, feats)

    sent = swap_cores(dot(near[1], w_all, ((1,), (1,))).astype(BF))
    partial_value = (dot(near[0], w_all, ((1,), (1,))) + sent.astype(jnp.float32)).astype(BF)
    partial_value = partial_value.reshape(4, pair, NX * cols)
    partial_value, cot = lax.optimization_barrier((partial_value, cot))
    parts = lax.all_to_all(partial_value, "yh", split_axis=0, concat_axis=0)
    hidden = jnp.sum(parts.astype(jnp.float32), axis=0)

    cot = in_order(shift_blocks(cot.reshape(NX, pair, cols), here), here)
    cot = cot.transpose(1, 0, 2).reshape(pair, NX * cols)

    activated, pullback = jax.vjp(gelu_tanh, hidden)
    hidden_grad = pullback(cot.astype(jnp.float32))[0].astype(BF)
    activated = activated.astype(BF)

    grad_own = lax.all_gather(hidden_grad, "yh", axis=0, tiled=True)
    grad_own, activated = lax.optimization_barrier((grad_own, activated))
    grad_other = swap_cores(grad_own)
    activated = swap_z_g(activated)

    ig_own = dot(grad_own, w_all, ((1,), (0,))).astype(BF)
    ig_own, grad_other = lax.optimization_barrier((ig_own, grad_other))
    ig_other = dot(grad_other, w_all, ((1,), (0,))).astype(BF)
    ig = jnp.stack([ig_own, ig_other]).reshape(16, rows, feats)
    ig, grad_own = lax.optimization_barrier((ig, grad_own))
    ig = exchange_rows(ig)
    input_grad = jnp.sum(ig.astype(jnp.float32), axis=0).astype(BF)

    far_own = grad_own.reshape(4 * pair, NX, cols).transpose(1, 0, 2)
    far_own = in_order(shift_blocks(far_own, here), here)
    far_own, activated = lax.optimization_barrier((far_own, activated))
    far_other = swap_cores(far_own)
    far = lax.all_gather(near, "x", axis=0, tiled=False)
    far_grad = jnp.stack([far_own, far_other], axis=1)
    weight_grad = dot(far.reshape(-1, feats), far_grad.reshape(-1, cols), ((0,), (0,))).astype(BF)

    activated = activated.reshape(pair, NX, cols).transpose(1, 0, 2)
    out = in_order(shift_blocks(activated, here), here).reshape(NX * pair, cols)
    return out, input_grad, weight_grad


def solution(mesh):
    fine = Mesh(mesh.devices.reshape(NX, 2, 8, 4, 2), AXES)
    in_specs = (P(("z", "x", "yl"), ("yh", "c")), P(("yh", "c"), ("x", "yl", "z")), P("z", ("x", "yl", "yh", "c")))
    out_specs = (in_specs[2], in_specs[0], in_specs[1])
    return jax.shard_map(body, mesh=fine, in_specs=in_specs, out_specs=out_specs, check_vma=False)
```

```python
import jax
import jax.numpy as jnp
from jax import lax
from jax.sharding import Mesh
from jax.sharding import PartitionSpec as P

AXES = ("x", "yl", "z", "yh", "c")
NX = 4
BF = jnp.bfloat16
GROUPS = [
    [(2 * h + (c ^ p)) * 4 + l * 2 + c for p in range(2) for h in range(4) for l in range(2)] for c in range(2)
]


def gelu_tanh(values):
    return jax.nn.gelu(values, approximate=True)


def along_x(value, shift):
    return lax.ppermute(value, "x", [(i, (i + shift) % NX) for i in range(NX)])


def swap_cores(value):
    return lax.ppermute(value, "c", [(0, 1), (1, 0)])


def swap_z_g(value):
    pairs = [(a * 8 + b, b * 8 + a) for a in range(8) for b in range(8)]
    return lax.ppermute(value, ("z", "yh", "c"), pairs)


def shift_blocks(blocks, here):
    parts = []
    for r in range(NX):
        block = lax.dynamic_index_in_dim(blocks, (here + r) & (NX - 1), 0, keepdims=False)
        parts.append(along_x(block, r) if r else block)
    return parts


def in_order(parts, here):
    out = jnp.zeros((NX,) + parts[0].shape, BF)
    for r in range(NX):
        out = lax.dynamic_update_index_in_dim(out, parts[r], (here + (NX - r)) & (NX - 1), 0)
    return out


def exchange_rows(value):
    return lax.all_to_all(
        value, ("z", "yl", "c"), split_axis=0, concat_axis=0, axis_index_groups=GROUPS
    )


def dot(a, b, contract):
    return lax.dot_general(a, b, (contract, ((), ())), preferred_element_type=jnp.float32)


def body(tokens, w_up, act_grad):
    rows, feats = tokens.shape
    cols = w_up.shape[1]
    pair = 2 * rows
    here = lax.axis_index("x").astype(jnp.uint32)

    w_all = lax.all_gather(w_up.T, "x", axis=0, tiled=False)

    near = exchange_rows(jnp.broadcast_to(tokens[None], (16, rows, feats)))
    near = near.reshape(2, 4 * pair, feats)

    near, cot, w_all = lax.optimization_barrier((near, swap_z_g(act_grad.T), w_all))
    w_all = w_all.reshape(NX * cols, feats)

    sent = swap_cores(dot(near[1], w_all, ((1,), (1,))).astype(BF))
    partial_value = (dot(near[0], w_all, ((1,), (1,))) + sent.astype(jnp.float32)).astype(BF)
    partial_value = partial_value.reshape(4, pair, NX * cols)
    partial_value, cot = lax.optimization_barrier((partial_value, cot))
    parts = lax.all_to_all(partial_value, "yh", split_axis=0, concat_axis=0)
    hidden = jnp.sum(parts.astype(jnp.float32), axis=0)

    cot = in_order(shift_blocks(cot.T.reshape(NX, pair, cols), here), here)
    cot = cot.transpose(1, 0, 2).reshape(pair, NX * cols)

    activated, pullback = jax.vjp(gelu_tanh, hidden)
    hidden_grad = pullback(cot.astype(jnp.float32))[0].astype(BF)
    activated = activated.astype(BF)

    grad_own = lax.all_gather(hidden_grad, "yh", axis=0, tiled=True)
    grad_own, activated = lax.optimization_barrier((grad_own, activated))
    both = jnp.concatenate([grad_own, activated], axis=0)
    both = both.reshape(5 * pair, NX, cols).transpose(1, 0, 2)
    both = shift_blocks(both, here)
    grad_other = swap_cores(grad_own)

    ig_own = dot(grad_own, w_all, ((1,), (0,))).astype(BF)
    ig_own, grad_other, *both = lax.optimization_barrier((ig_own, grad_other, *both))
    ig_other = dot(grad_other, w_all, ((1,), (0,))).astype(BF)
    ig = jnp.stack([ig_own, ig_other]).reshape(16, rows, feats)
    out = in_order([part[4 * pair :] for part in both], here).reshape(NX * pair, cols)
    ig, out, *both = lax.optimization_barrier((ig, out.T, *both))
    out = swap_z_g(out).T
    ig = exchange_rows(ig)
    input_grad = jnp.sum(ig.astype(jnp.float32), axis=0).astype(BF)

    far_own = in_order([part[: 4 * pair] for part in both], here)
    far_other = swap_cores(far_own)
    far = lax.all_gather(near, "x", axis=0, tiled=False)
    far_grad = jnp.stack([far_own, far_other], axis=1)
    weight_grad = dot(far.reshape(-1, feats), far_grad.reshape(-1, cols), ((0,), (0,))).astype(BF)
    return out, input_grad, weight_grad


def solution(mesh):
    fine = Mesh(mesh.devices.reshape(NX, 2, 8, 4, 2), AXES)
    in_specs = (P(("z", "x", "yl"), ("yh", "c")), P(("yh", "c"), ("x", "yl", "z")), P("z", ("x", "yl", "yh", "c")))
    out_specs = (in_specs[2], in_specs[0], in_specs[1])
    return jax.shard_map(body, mesh=fine, in_specs=in_specs, out_specs=out_specs, check_vma=False)
```

```python
import jax
import jax.numpy as jnp
from jax import lax
from jax.sharding import Mesh
from jax.sharding import PartitionSpec as P

AXES = ("x", "yl", "z", "yh", "c")
NX = 4
BF = jnp.bfloat16
GROUPS = [
    [(2 * h + (c ^ p)) * 4 + l * 2 + c for p in range(2) for h in range(4) for l in range(2)] for c in range(2)
]


def gelu_tanh(values):
    return jax.nn.gelu(values, approximate=True)


def along_x(value, shift):
    return lax.ppermute(value, "x", [(i, (i + shift) % NX) for i in range(NX)])


def swap_cores(value):
    return lax.ppermute(value, "c", [(0, 1), (1, 0)])


def swap_z_g(value):
    pairs = [(a * 8 + b, b * 8 + a) for a in range(8) for b in range(8)]
    return lax.ppermute(value, ("z", "yh", "c"), pairs)


def shift_blocks(blocks, here):
    parts = []
    for r in range(NX):
        block = lax.dynamic_index_in_dim(blocks, (here + r) & (NX - 1), 0, keepdims=False)
        parts.append(along_x(block, r) if r else block)
    return parts


def in_order(parts, here):
    out = jnp.zeros((NX,) + parts[0].shape, BF)
    for r in range(NX):
        out = lax.dynamic_update_index_in_dim(out, parts[r], (here + (NX - r)) & (NX - 1), 0)
    return out


def exchange_rows(value):
    return lax.all_to_all(
        value, ("z", "yl", "c"), split_axis=0, concat_axis=0, axis_index_groups=GROUPS
    )


def dot(a, b, contract):
    return lax.dot_general(a, b, (contract, ((), ())), preferred_element_type=jnp.float32)


def body(tokens, w_up, act_grad):
    rows, feats = tokens.shape
    cols = w_up.shape[1]
    pair = 2 * rows
    here = lax.axis_index("x").astype(jnp.uint32)

    w_all = lax.all_gather(w_up.T, "x", axis=0, tiled=False)

    near = exchange_rows(jnp.broadcast_to(tokens[None], (16, rows, feats)))
    near = near.reshape(2, 4 * pair, feats)

    near, cot, w_all = lax.optimization_barrier((near, swap_z_g(act_grad), w_all))
    w_all = w_all.reshape(NX * cols, feats)

    sent = swap_cores(dot(near[1], w_all, ((1,), (1,))).astype(BF))
    partial_value = (dot(near[0], w_all, ((1,), (1,))) + sent.astype(jnp.float32)).astype(BF)
    partial_value = partial_value.reshape(4, pair, NX * cols)
    partial_value, cot = lax.optimization_barrier((partial_value, cot))
    parts = lax.all_to_all(partial_value, "yh", split_axis=0, concat_axis=0)
    hidden = jnp.sum(parts.astype(jnp.float32), axis=0)

    cot = in_order(shift_blocks(cot.reshape(NX, pair, cols), here), here)
    cot = cot.transpose(1, 0, 2).reshape(pair, NX * cols)

    activated, pullback = jax.vjp(gelu_tanh, hidden)
    hidden_grad = pullback(cot.astype(jnp.float32))[0].astype(BF)
    activated = activated.astype(BF)

    grad_own = lax.all_gather(hidden_grad, "yh", axis=0, tiled=True)
    grad_own, activated = lax.optimization_barrier((grad_own, swap_z_g(activated)))
    grad_other = swap_cores(grad_own)

    ig_own = dot(grad_own, w_all, ((1,), (0,))).astype(BF)
    ig_own, grad_other = lax.optimization_barrier((ig_own, grad_other))
    ig_other = dot(grad_other, w_all, ((1,), (0,))).astype(BF)
    ig = jnp.stack([ig_own, ig_other]).reshape(16, rows, feats)
    ig = exchange_rows(ig)
    input_grad = jnp.sum(ig.astype(jnp.float32), axis=0).astype(BF)

    both = jnp.concatenate([grad_own, activated], axis=0)
    both = both.reshape(5 * pair, NX, cols).transpose(1, 0, 2)
    both = shift_blocks(both, here)
    far_own = in_order([part[: 4 * pair] for part in both], here)
    far_other = swap_cores(far_own)
    far = lax.all_gather(near, "x", axis=0, tiled=False)
    far_grad = jnp.stack([far_own, far_other], axis=1)
    weight_grad = dot(far.reshape(-1, feats), far_grad.reshape(-1, cols), ((0,), (0,))).astype(BF)
    out = in_order([part[4 * pair :] for part in both], here).reshape(NX * pair, cols)
    return out, input_grad, weight_grad


def solution(mesh):
    fine = Mesh(mesh.devices.reshape(NX, 2, 8, 4, 2), AXES)
    in_specs = (P(("z", "x", "yl"), ("yh", "c")), P(("yh", "c"), ("x", "yl", "z")), P("z", ("x", "yl", "yh", "c")))
    out_specs = (in_specs[2], in_specs[0], in_specs[1])
    return jax.shard_map(body, mesh=fine, in_specs=in_specs, out_specs=out_specs, check_vma=False)
```

```python
import jax
import jax.numpy as jnp
from jax import lax
from jax.sharding import Mesh
from jax.sharding import PartitionSpec as P

AXES = ("x", "yl", "z", "yh", "c")
NX = 4
BF = jnp.bfloat16


def gelu_tanh(values):
    return jax.nn.gelu(values, approximate=True)


def along_x(value, shift):
    return lax.ppermute(value, "x", [(i, (i + shift) % NX) for i in range(NX)])


def swap_cores(value):
    return lax.ppermute(value, "c", [(0, 1), (1, 0)])


def turn(core, high):
    return 4 * core + high


def along_z(value, sign):
    pairs = []
    for z in range(8):
        for g in range(8):
            pairs.append((z * 8 + g, (z + sign * turn(g % 2, g // 2)) % 8 * 8 + g))
    return lax.ppermute(value, ("z", "yh", "c"), pairs)


def within_z(value, home):
    pairs = []
    for z in range(8):
        for g in range(8):
            pair = (z * 8 + g, z * 8 + (z - turn(g % 2, g // 2)) % 8)
            pairs.append(pair if home else pair[::-1])
    return lax.ppermute(value, ("z", "yh", "c"), pairs)


def shift_blocks(blocks, here):
    parts = []
    for r in range(NX):
        block = lax.dynamic_index_in_dim(blocks, (here + r) & (NX - 1), 0, keepdims=False)
        parts.append(along_x(block, r) if r else block)
    return parts


def in_order(parts, here, out=None):
    out = jnp.zeros((NX,) + parts[0].shape, BF) if out is None else out
    for r in range(NX):
        out = lax.dynamic_update_index_in_dim(out, parts[r], (here + (NX - r)) & (NX - 1), 0)
    return out


def cut(blocks, start, count):
    n, m = blocks.shape[1:]
    twice = jnp.concatenate([blocks, blocks], axis=0).reshape(16 * n, m)
    return lax.dynamic_slice_in_dim(twice, (start & 7) * n, count * n, 0)


def dot(a, b, contract):
    return lax.dot_general(a, b, (contract, ((), ())), preferred_element_type=jnp.float32)


def body(tokens, w_up, act_grad):
    rows, feats = tokens.shape
    cols = w_up.shape[1]
    pair = 2 * rows
    here = lax.axis_index("x").astype(jnp.uint32)
    first = lax.axis_index("z").astype(jnp.uint32) + 4 * lax.axis_index("c").astype(jnp.uint32)

    w_own = w_up.T
    w_all = jnp.zeros((NX, cols, feats), BF)
    for r in range(NX):
        block = along_x(w_own, -r) if r else w_own
        w_all = lax.dynamic_update_index_in_dim(w_all, block, (here + r) & (NX - 1), 0)

    near = lax.all_gather(tokens, "yl", axis=0, tiled=True)
    near = lax.all_gather(near, "z", axis=0, tiled=False)
    near, cot = lax.optimization_barrier((near, within_z(act_grad, False)))
    near = jnp.stack([cut(near, first, 4), cut(near, first + 4, 4)])
    w_all = w_all.reshape(NX * cols, feats)

    sent = swap_cores(dot(near[1], w_all, ((1,), (1,))).astype(BF))
    partial_value = (dot(near[0], w_all, ((1,), (1,))) + sent.astype(jnp.float32)).astype(BF)
    partial_value = partial_value.reshape(4, pair, NX * cols)
    partial_value, cot = lax.optimization_barrier((partial_value, cot))
    parts = lax.all_to_all(partial_value, "yh", split_axis=0, concat_axis=0)
    hidden = jnp.sum(parts.astype(jnp.float32), axis=0)

    cot = along_z(cot, -1)
    cot = in_order(shift_blocks(cot.reshape(NX, pair, cols), here), here)
    cot = cot.transpose(1, 0, 2).reshape(pair, NX * cols)

    activated, pullback = jax.vjp(gelu_tanh, hidden)
    hidden_grad = pullback(cot.astype(jnp.float32))[0].astype(BF)
    activated = activated.astype(BF)

    grad_own = lax.all_gather(hidden_grad, "yh", axis=0, tiled=True)
    grad_own, activated = lax.optimization_barrier((grad_own, along_z(activated, 1)))
    grad_other = swap_cores(grad_own)
    activated = within_z(activated, True)

    ig_own = dot(grad_own, w_all, ((1,), (0,))).astype(BF)
    ig_own, grad_other = lax.optimization_barrier((ig_own, grad_other))
    ig_other = dot(grad_other, w_all, ((1,), (0,))).astype(BF)
    ig = cut(jnp.stack([ig_own, ig_other]).reshape(8, pair, feats), 16 - first, 8)
    far_own = jnp.zeros((NX, 4 * pair, cols), BF)
    ig, activated, far_own = lax.optimization_barrier((ig.reshape(16, rows, feats), activated, far_own))
    ig = lax.all_to_all(ig, ("z", "yl"), split_axis=0, concat_axis=0)
    input_grad = jnp.sum(ig.astype(jnp.float32), axis=0).astype(BF)

    blocks = grad_own.reshape(4 * pair, NX, cols).transpose(1, 0, 2)
    far_own = in_order(shift_blocks(blocks, here), here, far_own)
    far_other = swap_cores(far_own)
    far = lax.all_gather(near, "x", axis=0, tiled=False)
    far_grad = jnp.stack([far_own, far_other], axis=1)
    weight_grad = dot(far.reshape(-1, feats), far_grad.reshape(-1, cols), ((0,), (0,))).astype(BF)

    out = activated.reshape(pair, NX, cols).transpose(1, 0, 2)
    out = in_order(shift_blocks(out, here), here).reshape(NX * pair, cols)
    return out, input_grad, weight_grad


def solution(mesh):
    fine = Mesh(mesh.devices.reshape(NX, 2, 8, 4, 2), AXES)
    in_specs = (P(("z", "x", "yl"), ("yh", "c")), P(("yh", "c"), ("x", "yl", "z")), P("z", ("x", "yl", "yh", "c")))
    out_specs = (in_specs[2], in_specs[0], in_specs[1])
    return jax.shard_map(body, mesh=fine, in_specs=in_specs, out_specs=out_specs, check_vma=False)
```

```python
import jax
import jax.numpy as jnp
from jax import lax
from jax.sharding import Mesh
from jax.sharding import PartitionSpec as P

AXES = ("x", "yl", "z", "yh", "c")
NX = 4
BF = jnp.bfloat16


def gelu_tanh(values):
    return jax.nn.gelu(values, approximate=True)


def along_x(value, shift):
    return lax.ppermute(value, "x", [(i, (i + shift) % NX) for i in range(NX)])


def swap_cores(value):
    return lax.ppermute(value, "c", [(0, 1), (1, 0)])


def turn(core, high):
    return 4 * core + high


def along_z(value, sign):
    pairs = []
    for z in range(8):
        for g in range(8):
            pairs.append((z * 8 + g, (z + sign * turn(g % 2, g // 2)) % 8 * 8 + g))
    return lax.ppermute(value, ("z", "yh", "c"), pairs)


def within_z(value, home):
    pairs = []
    for z in range(8):
        for g in range(8):
            pair = (z * 8 + g, z * 8 + (z - turn(g % 2, g // 2)) % 8)
            pairs.append(pair if home else pair[::-1])
    return lax.ppermute(value, ("z", "yh", "c"), pairs)


def shift_blocks(blocks, here):
    parts = []
    for r in range(NX):
        block = lax.dynamic_index_in_dim(blocks, (here + r) & (NX - 1), 0, keepdims=False)
        parts.append(along_x(block, r) if r else block)
    return parts


def in_order(parts, here, out=None):
    out = jnp.zeros((NX,) + parts[0].shape, BF) if out is None else out
    for r in range(NX):
        out = lax.dynamic_update_index_in_dim(out, parts[r], (here + (NX - r)) & (NX - 1), 0)
    return out


def cut(blocks, start, count):
    n, m = blocks.shape[1:]
    twice = jnp.concatenate([blocks, blocks], axis=0).reshape(16 * n, m)
    return lax.dynamic_slice_in_dim(twice, (start & 7) * n, count * n, 0)


def dot(a, b, contract):
    return lax.dot_general(a, b, (contract, ((), ())), preferred_element_type=jnp.float32)


def body(tokens, w_up, act_grad):
    rows, feats = tokens.shape
    cols = w_up.shape[1]
    pair = 2 * rows
    here = lax.axis_index("x").astype(jnp.uint32)
    first = lax.axis_index("z").astype(jnp.uint32) + 4 * lax.axis_index("c").astype(jnp.uint32)

    w_all = lax.all_gather(w_up.T, "x", axis=0, tiled=False)

    near = jnp.broadcast_to(tokens[None], (16, rows, feats))
    near = lax.all_to_all(near, ("z", "yl"), split_axis=0, concat_axis=0).reshape(8, pair, feats)
    cot = along_z(within_z(act_grad, False), -1)
    near, cot, w_all = lax.optimization_barrier((near, cot, w_all))
    near = jnp.stack([cut(near, first, 4), cut(near, first + 4, 4)])
    w_all = w_all.reshape(NX * cols, feats)

    sent = swap_cores(dot(near[1], w_all, ((1,), (1,))).astype(BF))
    partial_value = (dot(near[0], w_all, ((1,), (1,))) + sent.astype(jnp.float32)).astype(BF)
    partial_value = partial_value.reshape(4, pair, NX * cols)
    partial_value, cot = lax.optimization_barrier((partial_value, cot))
    parts = lax.all_to_all(partial_value, "yh", split_axis=0, concat_axis=0)
    hidden = jnp.sum(parts.astype(jnp.float32), axis=0)

    cot = in_order(shift_blocks(cot.reshape(NX, pair, cols), here), here)
    cot = cot.transpose(1, 0, 2).reshape(pair, NX * cols)

    activated, pullback = jax.vjp(gelu_tanh, hidden)
    hidden_grad = pullback(cot.astype(jnp.float32))[0].astype(BF)
    activated = activated.astype(BF)

    grad_own = lax.all_gather(hidden_grad, "yh", axis=0, tiled=True)
    grad_own, activated = lax.optimization_barrier((grad_own, along_z(activated, 1)))
    grad_other = swap_cores(grad_own)

    ig_own = dot(grad_own, w_all, ((1,), (0,))).astype(BF)
    ig_own, grad_other = lax.optimization_barrier((ig_own, grad_other))
    ig_other = dot(grad_other, w_all, ((1,), (0,))).astype(BF)
    ig = cut(jnp.stack([ig_own, ig_other]).reshape(8, pair, feats), 16 - first, 8)
    ig, grad_own, activated = lax.optimization_barrier((ig.reshape(16, rows, feats), grad_own, activated))
    ig = lax.all_to_all(ig, ("z", "yl"), split_axis=0, concat_axis=0)

    far = lax.all_gather(near, "x", axis=0, tiled=False)
    far, grad_own, activated = lax.optimization_barrier((far, grad_own, activated))
    both = jnp.concatenate([grad_own, activated], axis=0)
    both = shift_blocks(both.reshape(5 * pair, NX, cols).transpose(1, 0, 2), here)
    far_own = in_order([part[: 4 * pair] for part in both], here)
    far_other = swap_cores(far_own)
    far_grad = jnp.stack([far_own, far_other], axis=1)
    weight_grad = dot(far.reshape(-1, feats), far_grad.reshape(-1, cols), ((0,), (0,))).astype(BF)
    out = in_order([part[4 * pair :] for part in both], here).reshape(NX * pair, cols)
    out = within_z(out, True)
    ig, weight_grad = lax.optimization_barrier((ig, weight_grad))
    input_grad = jnp.sum(ig.astype(jnp.float32), axis=0).astype(BF)
    return out, input_grad, weight_grad


def solution(mesh):
    fine = Mesh(mesh.devices.reshape(NX, 2, 8, 4, 2), AXES)
    in_specs = (P(("z", "x", "yl"), ("yh", "c")), P(("yh", "c"), ("x", "yl", "z")), P("z", ("x", "yl", "yh", "c")))
    out_specs = (in_specs[2], in_specs[0], in_specs[1])
    return jax.shard_map(body, mesh=fine, in_specs=in_specs, out_specs=out_specs, check_vma=False)
```

```python
import jax
import jax.numpy as jnp
from jax import lax
from jax.sharding import Mesh
from jax.sharding import PartitionSpec as P

AXES = ("x", "yl", "z", "yh", "c")
NX = 4
BF = jnp.bfloat16


def gelu_tanh(values):
    return jax.nn.gelu(values, approximate=True)


def along_x(value, shift):
    return lax.ppermute(value, "x", [(i, (i + shift) % NX) for i in range(NX)])


def swap_cores(value):
    return lax.ppermute(value, "c", [(0, 1), (1, 0)])


def turn(core, high):
    return 4 * core + high


def along_z(value, sign):
    pairs = []
    for z in range(8):
        for g in range(8):
            pairs.append((z * 8 + g, (z + sign * turn(g % 2, g // 2)) % 8 * 8 + g))
    return lax.ppermute(value, ("z", "yh", "c"), pairs)


def within_z(value, home):
    pairs = []
    for z in range(8):
        for g in range(8):
            pair = (z * 8 + g, z * 8 + (z - turn(g % 2, g // 2)) % 8)
            pairs.append(pair if home else pair[::-1])
    return lax.ppermute(value, ("z", "yh", "c"), pairs)


def shift_blocks(blocks, here):
    parts = []
    for r in range(NX):
        block = lax.dynamic_index_in_dim(blocks, (here + r) & (NX - 1), 0, keepdims=False)
        parts.append(along_x(block, r) if r else block)
    return parts


def in_order(parts, here, out=None):
    out = jnp.zeros((NX,) + parts[0].shape, BF) if out is None else out
    for r in range(NX):
        out = lax.dynamic_update_index_in_dim(out, parts[r], (here + (NX - r)) & (NX - 1), 0)
    return out


def cut(blocks, start, count):
    n, m = blocks.shape[1:]
    twice = jnp.concatenate([blocks, blocks], axis=0).reshape(16 * n, m)
    return lax.dynamic_slice_in_dim(twice, (start & 7) * n, count * n, 0)


def dot(a, b, contract):
    return lax.dot_general(a, b, (contract, ((), ())), preferred_element_type=jnp.float32)


def body(tokens, w_up, act_grad):
    rows, feats = tokens.shape
    cols = w_up.shape[1]
    pair = 2 * rows
    here = lax.axis_index("x").astype(jnp.uint32)
    first = lax.axis_index("z").astype(jnp.uint32) + 4 * lax.axis_index("c").astype(jnp.uint32)

    w_all = lax.all_gather(w_up.T, "x", axis=0, tiled=False)

    near = jnp.broadcast_to(tokens[None], (16, rows, feats))
    near = lax.all_to_all(near, ("z", "yl"), split_axis=0, concat_axis=0).reshape(8, pair, feats)
    cot = along_z(within_z(act_grad, False), -1)
    near, cot, w_all = lax.optimization_barrier((near, cot, w_all))
    near = jnp.stack([cut(near, first, 4), cut(near, first + 4, 4)])
    w_all = w_all.reshape(NX * cols, feats)

    sent = swap_cores(dot(near[1], w_all, ((1,), (1,))).astype(BF))
    partial_value = (dot(near[0], w_all, ((1,), (1,))) + sent.astype(jnp.float32)).astype(BF)
    partial_value = partial_value.reshape(4, pair, NX * cols)
    partial_value, cot = lax.optimization_barrier((partial_value, cot))
    parts = lax.all_to_all(partial_value, "yh", split_axis=0, concat_axis=0)
    hidden = jnp.sum(parts.astype(jnp.float32), axis=0)

    cot = in_order(shift_blocks(cot.reshape(NX, pair, cols), here), here)
    cot = cot.transpose(1, 0, 2).reshape(pair, NX * cols)

    activated, pullback = jax.vjp(gelu_tanh, hidden)
    hidden_grad = pullback(cot.astype(jnp.float32))[0].astype(BF)
    activated = activated.astype(BF)

    grad_own = lax.all_gather(hidden_grad, "yh", axis=0, tiled=True)
    grad_own, activated = lax.optimization_barrier((grad_own, along_z(activated, 1)))
    grad_other = swap_cores(grad_own)

    ig_own = dot(grad_own, w_all, ((1,), (0,))).astype(BF)
    ig_own, grad_other = lax.optimization_barrier((ig_own, grad_other))
    ig_other = dot(grad_other, w_all, ((1,), (0,))).astype(BF)
    ig = cut(jnp.stack([ig_own, ig_other]).reshape(8, pair, feats), 16 - first, 8)
    ig, grad_own, activated = lax.optimization_barrier((ig.reshape(16, rows, feats), grad_own, activated))
    ig = lax.all_to_all(ig, ("z", "yl"), split_axis=0, concat_axis=0)

    far = lax.all_gather(near, "x", axis=0, tiled=False)
    far, grad_own, activated = lax.optimization_barrier((far, grad_own, activated))
    both = jnp.concatenate([grad_own, activated], axis=0)
    both = shift_blocks(both.reshape(5 * pair, NX, cols).transpose(1, 0, 2), here)
    far_own = in_order([part[: 4 * pair] for part in both], here)
    far_other = swap_cores(far_own)
    far_grad = jnp.stack([far_own, far_other], axis=1)
    weight_grad = dot(far.reshape(-1, feats), far_grad.reshape(-1, cols), ((0,), (0,))).astype(BF)
    out = in_order([part[4 * pair :] for part in both], here).reshape(NX * pair, cols)
    ig, weight_grad, out = lax.optimization_barrier((ig, weight_grad, within_z(out, True)))
    input_grad = jnp.sum(ig.astype(jnp.float32), axis=0).astype(BF)
    return out, input_grad, weight_grad


def solution(mesh):
    fine = Mesh(mesh.devices.reshape(NX, 2, 8, 4, 2), AXES)
    in_specs = (P(("z", "x", "yl"), ("yh", "c")), P(("yh", "c"), ("x", "yl", "z")), P("z", ("x", "yl", "yh", "c")))
    out_specs = (in_specs[2], in_specs[0], in_specs[1])
    return jax.shard_map(body, mesh=fine, in_specs=in_specs, out_specs=out_specs, check_vma=False)
```

```python
import jax
import jax.numpy as jnp
from jax import lax
from jax.sharding import Mesh
from jax.sharding import PartitionSpec as P

AXES = ("x", "yl", "z", "yh", "c")
NX = 4
BF = jnp.bfloat16


def gelu_tanh(values):
    return jax.nn.gelu(values, approximate=True)


def along_x(value, shift):
    return lax.ppermute(value, "x", [(i, (i + shift) % NX) for i in range(NX)])


def swap_cores(value):
    return lax.ppermute(value, "c", [(0, 1), (1, 0)])


def turn(core, high):
    return 4 * core + high


def along_z(value, sign):
    pairs = []
    for z in range(8):
        for g in range(8):
            pairs.append((z * 8 + g, (z + sign * turn(g % 2, g // 2)) % 8 * 8 + g))
    return lax.ppermute(value, ("z", "yh", "c"), pairs)


def within_z(value, home):
    pairs = []
    for z in range(8):
        for g in range(8):
            pair = (z * 8 + g, z * 8 + (z - turn(g % 2, g // 2)) % 8)
            pairs.append(pair if home else pair[::-1])
    return lax.ppermute(value, ("z", "yh", "c"), pairs)


def shift_blocks(blocks, here):
    parts = []
    for r in range(NX):
        block = lax.dynamic_index_in_dim(blocks, (here + r) & (NX - 1), 0, keepdims=False)
        parts.append(along_x(block, r) if r else block)
    return parts


def in_order(parts, here, out=None):
    out = jnp.zeros((NX,) + parts[0].shape, BF) if out is None else out
    for r in range(NX):
        out = lax.dynamic_update_index_in_dim(out, parts[r], (here + (NX - r)) & (NX - 1), 0)
    return out


def cut(blocks, start, count):
    n, m = blocks.shape[1:]
    twice = jnp.concatenate([blocks, blocks], axis=0).reshape(16 * n, m)
    return lax.dynamic_slice_in_dim(twice, (start & 7) * n, count * n, 0)


def dot(a, b, contract):
    return lax.dot_general(a, b, (contract, ((), ())), preferred_element_type=jnp.float32)


def body(tokens, w_up, act_grad):
    rows, feats = tokens.shape
    cols = w_up.shape[1]
    pair = 2 * rows
    here = lax.axis_index("x").astype(jnp.uint32)
    first = lax.axis_index("z").astype(jnp.uint32) + 4 * lax.axis_index("c").astype(jnp.uint32)

    w_all = lax.all_gather(w_up.T, "x", axis=0, tiled=False)

    near = jnp.broadcast_to(tokens[None], (16, rows, feats))
    near = lax.all_to_all(near, ("z", "yl"), split_axis=0, concat_axis=0).reshape(8, pair, feats)
    cot = along_z(within_z(act_grad, False), -1)
    near, cot, w_all = lax.optimization_barrier((near, cot, w_all))
    near = jnp.stack([cut(near, first, 4), cut(near, first + 4, 4)])
    w_all = w_all.reshape(NX * cols, feats)

    sent = swap_cores(dot(near[1], w_all, ((1,), (1,))).astype(BF))
    partial_value = (dot(near[0], w_all, ((1,), (1,))) + sent.astype(jnp.float32)).astype(BF)
    partial_value = partial_value.reshape(4, pair, NX * cols)
    partial_value, cot = lax.optimization_barrier((partial_value, cot))
    parts = lax.all_to_all(partial_value, "yh", split_axis=0, concat_axis=0)
    hidden = jnp.sum(parts.astype(jnp.float32), axis=0)

    cot = in_order(shift_blocks(cot.reshape(NX, pair, cols), here), here)
    cot = cot.transpose(1, 0, 2).reshape(pair, NX * cols)

    activated, pullback = jax.vjp(gelu_tanh, hidden)
    hidden_grad = pullback(cot.astype(jnp.float32))[0].astype(BF)
    activated = activated.astype(BF)

    both = jnp.concatenate([hidden_grad, activated], axis=0)
    both = lax.optimization_barrier(both.reshape(2 * pair, NX, cols).transpose(1, 0, 2))
    both = shift_blocks(both, here)
    grad_own = lax.all_gather(hidden_grad, "yh", axis=0, tiled=True)
    grad_own, *both = lax.optimization_barrier((grad_own, *both))
    grad_other = swap_cores(grad_own)
    both = in_order(both, here)
    out = along_z(both[:, pair:].reshape(NX * pair, cols), 1)

    ig_own = dot(grad_own, w_all, ((1,), (0,))).astype(BF)
    ig_own, grad_other = lax.optimization_barrier((ig_own, grad_other))
    ig_other = dot(grad_other, w_all, ((1,), (0,))).astype(BF)
    ig = cut(jnp.stack([ig_own, ig_other]).reshape(8, pair, feats), 16 - first, 8)
    far_own = both[:, :pair]
    ig, far_own = lax.optimization_barrier((ig.reshape(16, rows, feats), far_own))
    ig = lax.all_to_all(ig, ("z", "yl"), split_axis=0, concat_axis=0)

    far_own, out = lax.optimization_barrier((far_own, out))
    out = within_z(out, True)
    far_own = lax.all_gather(far_own, "yh", axis=0, tiled=False)
    far_own, out = lax.optimization_barrier((far_own, out))
    far_other = swap_cores(far_own)
    far_grad = jnp.stack([far_own, far_other]).transpose(2, 0, 1, 3, 4)
    far = lax.all_gather(near, "x", axis=0, tiled=False)
    weight_grad = dot(far.reshape(-1, feats), far_grad.reshape(-1, cols), ((0,), (0,))).astype(BF)
    ig, weight_grad = lax.optimization_barrier((ig, weight_grad))
    input_grad = jnp.sum(ig.astype(jnp.float32), axis=0).astype(BF)
    return out, input_grad, weight_grad


def solution(mesh):
    fine = Mesh(mesh.devices.reshape(NX, 2, 8, 4, 2), AXES)
    in_specs = (P(("z", "x", "yl"), ("yh", "c")), P(("yh", "c"), ("x", "yl", "z")), P("z", ("x", "yl", "yh", "c")))
    out_specs = (in_specs[2], in_specs[0], in_specs[1])
    return jax.shard_map(body, mesh=fine, in_specs=in_specs, out_specs=out_specs, check_vma=False)
```

```python
import jax
import jax.numpy as jnp
from jax import lax
from jax.sharding import Mesh
from jax.sharding import PartitionSpec as P

AXES = ("x", "yl", "z", "yh", "c")
NX = 4
BF = jnp.bfloat16


def gelu_tanh(values):
    return jax.nn.gelu(values, approximate=True)


def along_x(value, shift):
    return lax.ppermute(value, "x", [(i, (i + shift) % NX) for i in range(NX)])


def swap_cores(value):
    return lax.ppermute(value, "c", [(0, 1), (1, 0)])


def turn(core, high):
    return 4 * core + high


def along_z(value, sign):
    pairs = []
    for z in range(8):
        for g in range(8):
            pairs.append((z * 8 + g, (z + sign * turn(g % 2, g // 2)) % 8 * 8 + g))
    return lax.ppermute(value, ("z", "yh", "c"), pairs)


def within_z(value, home):
    pairs = []
    for z in range(8):
        for g in range(8):
            pair = (z * 8 + g, z * 8 + (z - turn(g % 2, g // 2)) % 8)
            pairs.append(pair if home else pair[::-1])
    return lax.ppermute(value, ("z", "yh", "c"), pairs)


def shift_blocks(blocks, here):
    parts = []
    for r in range(NX):
        block = lax.dynamic_index_in_dim(blocks, (here + r) & (NX - 1), 0, keepdims=False)
        parts.append(along_x(block, r) if r else block)
    return parts


def in_order(parts, here, out=None):
    out = jnp.zeros((NX,) + parts[0].shape, BF) if out is None else out
    for r in range(NX):
        out = lax.dynamic_update_index_in_dim(out, parts[r], (here + (NX - r)) & (NX - 1), 0)
    return out


def cut(blocks, start, count):
    n, m = blocks.shape[1:]
    twice = jnp.concatenate([blocks, blocks], axis=0).reshape(16 * n, m)
    return lax.dynamic_slice_in_dim(twice, (start & 7) * n, count * n, 0)


def dot(a, b, contract):
    return lax.dot_general(a, b, (contract, ((), ())), preferred_element_type=jnp.float32)


def body(tokens, w_up, act_grad):
    rows, feats = tokens.shape
    cols = w_up.shape[1]
    pair = 2 * rows
    here = lax.axis_index("x").astype(jnp.uint32)
    first = lax.axis_index("z").astype(jnp.uint32) + 4 * lax.axis_index("c").astype(jnp.uint32)

    w_all = lax.all_gather(w_up.T, "x", axis=0, tiled=False)

    near = jnp.broadcast_to(tokens[None], (16, rows, feats))
    near = lax.all_to_all(near, ("z", "yl"), split_axis=0, concat_axis=0).reshape(8, pair, feats)
    cot = along_z(within_z(act_grad, False), -1)
    near, cot, w_all = lax.optimization_barrier((near, cot, w_all))
    near = jnp.stack([cut(near, first, 4), cut(near, first + 4, 4)])
    w_all = w_all.reshape(NX * cols, feats)

    sent = swap_cores(dot(near[1], w_all, ((1,), (1,))).astype(BF))
    partial_value = (dot(near[0], w_all, ((1,), (1,))) + sent.astype(jnp.float32)).astype(BF)
    partial_value = partial_value.reshape(4, pair, NX * cols)
    partial_value, cot = lax.optimization_barrier((partial_value, cot))
    parts = lax.all_to_all(partial_value, "yh", split_axis=0, concat_axis=0)
    hidden = jnp.sum(parts.astype(jnp.float32), axis=0)

    cot = in_order(shift_blocks(cot.reshape(NX, pair, cols), here), here)
    cot = cot.transpose(1, 0, 2).reshape(pair, NX * cols)

    activated, pullback = jax.vjp(gelu_tanh, hidden)
    hidden_grad = pullback(cot.astype(jnp.float32))[0].astype(BF)
    activated = activated.astype(BF)

    grad_own = lax.all_gather(hidden_grad, "yh", axis=0, tiled=True)
    grad_own, activated = lax.optimization_barrier((grad_own, along_z(activated, 1)))
    grad_other = swap_cores(grad_own)
    activated = within_z(activated, True)

    ig_own = dot(grad_own, w_all, ((1,), (0,))).astype(BF)
    ig_own, grad_other = lax.optimization_barrier((ig_own, grad_other))
    ig_other = dot(grad_other, w_all, ((1,), (0,))).astype(BF)
    ig = cut(jnp.stack([ig_own, ig_other]).reshape(8, pair, feats), 16 - first, 8)
    ig, grad_own = lax.optimization_barrier((ig.reshape(16, rows, feats), grad_own))
    ig = lax.all_to_all(ig, ("z", "yl"), split_axis=0, concat_axis=0)

    far = lax.all_gather(near, "x", axis=0, tiled=False)
    far, grad_own, activated = lax.optimization_barrier((far, grad_own, activated))
    both = jnp.concatenate([grad_own, activated], axis=0)
    both = shift_blocks(both.reshape(5 * pair, NX, cols).transpose(1, 0, 2), here)
    far_own = in_order([part[: 4 * pair] for part in both], here)
    far_other = swap_cores(far_own)
    far_grad = jnp.stack([far_own, far_other], axis=1)
    weight_grad = dot(far.reshape(-1, feats), far_grad.reshape(-1, cols), ((0,), (0,))).astype(BF)
    out = in_order([part[4 * pair :] for part in both], here).reshape(NX * pair, cols)
    ig, weight_grad, out = lax.optimization_barrier((ig, weight_grad, out))
    input_grad = jnp.sum(ig.astype(jnp.float32), axis=0).astype(BF)
    return out, input_grad, weight_grad


def solution(mesh):
    fine = Mesh(mesh.devices.reshape(NX, 2, 8, 4, 2), AXES)
    in_specs = (P(("z", "x", "yl"), ("yh", "c")), P(("yh", "c"), ("x", "yl", "z")), P("z", ("x", "yl", "yh", "c")))
    out_specs = (in_specs[2], in_specs[0], in_specs[1])
    return jax.shard_map(body, mesh=fine, in_specs=in_specs, out_specs=out_specs, check_vma=False)
```

```python
import jax
import jax.numpy as jnp
from jax import lax
from jax.sharding import Mesh
from jax.sharding import PartitionSpec as P

AXES = ("x", "yl", "z", "yh", "c")
NX = 4
SPLIT = 512
BF = jnp.bfloat16


def gelu_tanh(values):
    return jax.nn.gelu(values, approximate=True)


def along_x(value, shift):
    return lax.ppermute(value, "x", [(i, (i + shift) % NX) for i in range(NX)])


def swap_cores(value):
    return lax.ppermute(value, "c", [(0, 1), (1, 0)])


def turn(core, high):
    return 4 * core + high


def along_z(value, sign):
    pairs = []
    for z in range(8):
        for g in range(8):
            pairs.append((z * 8 + g, (z + sign * turn(g % 2, g // 2)) % 8 * 8 + g))
    return lax.ppermute(value, ("z", "yh", "c"), pairs)


def within_z(value, home):
    pairs = []
    for z in range(8):
        for g in range(8):
            pair = (z * 8 + g, z * 8 + (z - turn(g % 2, g // 2)) % 8)
            pairs.append(pair if home else pair[::-1])
    return lax.ppermute(value, ("z", "yh", "c"), pairs)


def shift_blocks(blocks, here):
    parts = []
    for r in range(NX):
        block = lax.dynamic_index_in_dim(blocks, (here + r) & (NX - 1), 0, keepdims=False)
        parts.append(along_x(block, r) if r else block)
    return parts


def in_order(parts, here, out=None):
    out = jnp.zeros((NX,) + parts[0].shape, BF) if out is None else out
    for r in range(NX):
        out = lax.dynamic_update_index_in_dim(out, parts[r], (here + (NX - r)) & (NX - 1), 0)
    return out


def cut(blocks, start, count):
    n, m = blocks.shape[1:]
    twice = jnp.concatenate([blocks, blocks], axis=0).reshape(16 * n, m)
    return lax.dynamic_slice_in_dim(twice, (start & 7) * n, count * n, 0)


def dot(a, b, contract):
    return lax.dot_general(a, b, (contract, ((), ())), preferred_element_type=jnp.float32)


def body(tokens, w_up, act_grad):
    rows, feats = tokens.shape
    cols = w_up.shape[1]
    pair = 2 * rows
    here = lax.axis_index("x").astype(jnp.uint32)
    first = lax.axis_index("z").astype(jnp.uint32) + 4 * lax.axis_index("c").astype(jnp.uint32)

    w_low = lax.all_gather(w_up.T[:, :SPLIT], "x", axis=0, tiled=True)
    w_own = w_up.T[:, SPLIT:]
    w_high = jnp.zeros((NX,) + w_own.shape, BF)
    for r in range(NX):
        block = along_x(w_own, -r) if r else w_own
        w_high = lax.dynamic_update_index_in_dim(w_high, block, (here + r) & (NX - 1), 0)
    w_high = w_high.reshape(NX * cols, feats - SPLIT)

    near = jnp.broadcast_to(tokens[None], (16, rows, feats))
    near = lax.all_to_all(near, ("z", "yl"), split_axis=0, concat_axis=0).reshape(8, pair, feats)
    near, cot = lax.optimization_barrier((near, within_z(act_grad, False)))
    cot = along_z(cot, -1)
    near = jnp.stack([cut(near, first, 4), cut(near, first + 4, 4)])

    def hidden_part(part):
        low = dot(part[:, :SPLIT], w_low, ((1,), (1,)))
        return low + dot(part[:, SPLIT:], w_high, ((1,), (1,)))

    sent = swap_cores(hidden_part(near[1]).astype(BF))
    partial_value = (hidden_part(near[0]) + sent.astype(jnp.float32)).astype(BF)
    partial_value = partial_value.reshape(4, pair, NX * cols)
    partial_value, w_low, w_high = lax.optimization_barrier((partial_value, w_low, w_high))
    w_all = jnp.concatenate([w_low, w_high], axis=1)
    parts = lax.all_to_all(partial_value, "yh", split_axis=0, concat_axis=0)
    hidden = jnp.sum(parts.astype(jnp.float32), axis=0)

    cot = in_order(shift_blocks(cot.reshape(NX, pair, cols), here), here)
    cot = cot.transpose(1, 0, 2).reshape(pair, NX * cols)
    cot, w_all = lax.optimization_barrier((cot, w_all))

    activated, pullback = jax.vjp(gelu_tanh, hidden)
    hidden_grad = pullback(cot.astype(jnp.float32))[0].astype(BF)
    activated = activated.astype(BF)

    grad_own = lax.all_gather(hidden_grad, "yh", axis=0, tiled=True)
    grad_own, activated = lax.optimization_barrier((grad_own, along_z(activated, 1)))
    grad_other = swap_cores(grad_own)
    activated = within_z(activated, True)

    ig_own = dot(grad_own, w_all, ((1,), (0,))).astype(BF)
    ig_own, grad_other = lax.optimization_barrier((ig_own, grad_other))
    ig_other = dot(grad_other, w_all, ((1,), (0,))).astype(BF)
    ig = cut(jnp.stack([ig_own, ig_other]).reshape(8, pair, feats), 16 - first, 8)
    ig, grad_own = lax.optimization_barrier((ig.reshape(16, rows, feats), grad_own))
    ig = lax.all_to_all(ig, ("z", "yl"), split_axis=0, concat_axis=0)

    far = lax.all_gather(near, "x", axis=0, tiled=False)
    far, grad_own, activated = lax.optimization_barrier((far, grad_own, activated))
    both = jnp.concatenate([grad_own, activated], axis=0)
    both = shift_blocks(both.reshape(5 * pair, NX, cols).transpose(1, 0, 2), here)
    far_own = in_order([part[: 4 * pair] for part in both], here)
    far_other = swap_cores(far_own)
    far_grad = jnp.stack([far_own, far_other], axis=1)
    weight_grad = dot(far.reshape(-1, feats), far_grad.reshape(-1, cols), ((0,), (0,))).astype(BF)
    out = in_order([part[4 * pair :] for part in both], here).reshape(NX * pair, cols)
    ig, weight_grad, out = lax.optimization_barrier((ig, weight_grad, out))
    input_grad = jnp.sum(ig.astype(jnp.float32), axis=0).astype(BF)
    return out, input_grad, weight_grad


def solution(mesh):
    fine = Mesh(mesh.devices.reshape(NX, 2, 8, 4, 2), AXES)
    in_specs = (P(("z", "x", "yl"), ("yh", "c")), P(("yh", "c"), ("x", "yl", "z")), P("z", ("x", "yl", "yh", "c")))
    out_specs = (in_specs[2], in_specs[0], in_specs[1])
    return jax.shard_map(body, mesh=fine, in_specs=in_specs, out_specs=out_specs, check_vma=False)
```

```python
import jax
import jax.numpy as jnp
from jax import lax
from jax.sharding import Mesh
from jax.sharding import PartitionSpec as P

AXES = ("x", "yl", "z", "yh", "c")
NX = 4
BF = jnp.bfloat16


def gelu_tanh(values):
    return jax.nn.gelu(values, approximate=True)


def along_x(value, shift):
    return lax.ppermute(value, "x", [(i, (i + shift) % NX) for i in range(NX)])


def swap_cores(value):
    return lax.ppermute(value, "c", [(0, 1), (1, 0)])


def turn(core, high):
    return 4 * core + high


def along_z(value, sign):
    pairs = []
    for z in range(8):
        for g in range(8):
            pairs.append((z * 8 + g, (z + sign * turn(g % 2, g // 2)) % 8 * 8 + g))
    return lax.ppermute(value, ("z", "yh", "c"), pairs)


def within_z(value, home):
    pairs = []
    for z in range(8):
        for g in range(8):
            pair = (z * 8 + g, z * 8 + (z - turn(g % 2, g // 2)) % 8)
            pairs.append(pair if home else pair[::-1])
    return lax.ppermute(value, ("z", "yh", "c"), pairs)


def shift_blocks(blocks, here):
    parts = []
    for r in range(NX):
        block = lax.dynamic_index_in_dim(blocks, (here + r) & (NX - 1), 0, keepdims=False)
        parts.append(along_x(block, r) if r else block)
    return parts


def in_order(parts, here, out=None):
    out = jnp.zeros((NX,) + parts[0].shape, BF) if out is None else out
    for r in range(NX):
        out = lax.dynamic_update_index_in_dim(out, parts[r], (here + (NX - r)) & (NX - 1), 0)
    return out


def cut(blocks, start, count):
    n, m = blocks.shape[1:]
    twice = jnp.concatenate([blocks, blocks], axis=0).reshape(16 * n, m)
    return lax.dynamic_slice_in_dim(twice, (start & 7) * n, count * n, 0)


def dot(a, b, contract):
    return lax.dot_general(a, b, (contract, ((), ())), preferred_element_type=jnp.float32)


def body(tokens, w_up, act_grad):
    rows, feats = tokens.shape
    cols = w_up.shape[1]
    pair = 2 * rows
    here = lax.axis_index("x").astype(jnp.uint32)
    first = lax.axis_index("z").astype(jnp.uint32) + 4 * lax.axis_index("c").astype(jnp.uint32)

    w_all = lax.all_gather(w_up.T, "x", axis=0, tiled=False)

    near = jnp.broadcast_to(tokens[None], (16, rows, feats))
    near = lax.all_to_all(near, ("z", "yl"), split_axis=0, concat_axis=0).reshape(8, pair, feats)
    cot = along_z(within_z(act_grad, False), -1)
    near, cot = lax.optimization_barrier((near, cot))
    near = jnp.stack([cut(near, first, 4), cut(near, first + 4, 4)])
    w_all = w_all.reshape(NX * cols, feats)

    sent = swap_cores(dot(near[1], w_all, ((1,), (1,))).astype(BF))
    partial_value, sent = lax.optimization_barrier((dot(near[0], w_all, ((1,), (1,))), sent))
    partial_value = (partial_value + sent.astype(jnp.float32)).astype(BF)
    partial_value = partial_value.reshape(4, pair, NX * cols)
    partial_value, cot = lax.optimization_barrier((partial_value, cot))
    parts = lax.all_to_all(partial_value, "yh", split_axis=0, concat_axis=0)
    hidden = jnp.sum(parts.astype(jnp.float32), axis=0)

    cot = in_order(shift_blocks(cot.reshape(NX, pair, cols), here), here)
    cot = cot.transpose(1, 0, 2).reshape(pair, NX * cols)

    activated, pullback = jax.vjp(gelu_tanh, hidden)
    hidden_grad = pullback(cot.astype(jnp.float32))[0].astype(BF)
    activated = activated.astype(BF)

    grad_own = lax.all_gather(hidden_grad, "yh", axis=0, tiled=True)
    grad_own, activated = lax.optimization_barrier((grad_own, along_z(activated, 1)))
    grad_other = swap_cores(grad_own)
    activated = within_z(activated, True)

    ig_own = dot(grad_own, w_all, ((1,), (0,))).astype(BF)
    ig_own, grad_other = lax.optimization_barrier((ig_own, grad_other))
    ig_other = dot(grad_other, w_all, ((1,), (0,))).astype(BF)
    ig = cut(jnp.stack([ig_own, ig_other]).reshape(8, pair, feats), 16 - first, 8)
    ig, grad_own = lax.optimization_barrier((ig.reshape(16, rows, feats), grad_own))
    ig = lax.all_to_all(ig, ("z", "yl"), split_axis=0, concat_axis=0)

    far = lax.all_gather(near, "x", axis=0, tiled=False)
    far, grad_own, activated = lax.optimization_barrier((far, grad_own, activated))
    both = jnp.concatenate([grad_own, activated], axis=0)
    both = shift_blocks(both.reshape(5 * pair, NX, cols).transpose(1, 0, 2), here)
    far_own = in_order([part[: 4 * pair] for part in both], here)
    far_other = swap_cores(far_own)
    far_grad = jnp.stack([far_own, far_other], axis=1)
    weight_grad = dot(far.reshape(-1, feats), far_grad.reshape(-1, cols), ((0,), (0,))).astype(BF)
    out = in_order([part[4 * pair :] for part in both], here).reshape(NX * pair, cols)
    ig, weight_grad, out = lax.optimization_barrier((ig, weight_grad, out))
    input_grad = jnp.sum(ig.astype(jnp.float32), axis=0).astype(BF)
    return out, input_grad, weight_grad


def solution(mesh):
    fine = Mesh(mesh.devices.reshape(NX, 2, 8, 4, 2), AXES)
    in_specs = (P(("z", "x", "yl"), ("yh", "c")), P(("yh", "c"), ("x", "yl", "z")), P("z", ("x", "yl", "yh", "c")))
    out_specs = (in_specs[2], in_specs[0], in_specs[1])
    return jax.shard_map(body, mesh=fine, in_specs=in_specs, out_specs=out_specs, check_vma=False)
```

```python
import jax
import jax.numpy as jnp
from jax import lax
from jax.sharding import Mesh
from jax.sharding import PartitionSpec as P

AXES = ("x", "yl", "z", "yh", "c")
NX = 4
BF = jnp.bfloat16


def gelu_tanh(values):
    return jax.nn.gelu(values, approximate=True)


def along_x(value, shift):
    return lax.ppermute(value, "x", [(i, (i + shift) % NX) for i in range(NX)])


def swap_cores(value):
    return lax.ppermute(value, "c", [(0, 1), (1, 0)])


def turn(core, high):
    return 4 * core + high


def along_z(value, sign):
    pairs = []
    for z in range(8):
        for g in range(8):
            pairs.append((z * 8 + g, (z + sign * turn(g % 2, g // 2)) % 8 * 8 + g))
    return lax.ppermute(value, ("z", "yh", "c"), pairs)


def within_z(value, home):
    pairs = []
    for z in range(8):
        for g in range(8):
            pair = (z * 8 + g, z * 8 + (z - turn(g % 2, g // 2)) % 8)
            pairs.append(pair if home else pair[::-1])
    return lax.ppermute(value, ("z", "yh", "c"), pairs)


def shift_blocks(blocks, here):
    parts = []
    for r in range(NX):
        block = lax.dynamic_index_in_dim(blocks, (here + r) & (NX - 1), 0, keepdims=False)
        parts.append(along_x(block, r) if r else block)
    return parts


def in_order(parts, here, out=None):
    out = jnp.zeros((NX,) + parts[0].shape, BF) if out is None else out
    for r in range(NX):
        out = lax.dynamic_update_index_in_dim(out, parts[r], (here + (NX - r)) & (NX - 1), 0)
    return out


def cut(blocks, start, count):
    n, m = blocks.shape[1:]
    twice = jnp.concatenate([blocks, blocks], axis=0).reshape(16 * n, m)
    return lax.dynamic_slice_in_dim(twice, (start & 7) * n, count * n, 0)


def dot(a, b, contract):
    return lax.dot_general(a, b, (contract, ((), ())), preferred_element_type=jnp.float32)


def body(tokens, w_up, act_grad):
    rows, feats = tokens.shape
    cols = w_up.shape[1]
    pair = 2 * rows
    here = lax.axis_index("x").astype(jnp.uint32)
    first = lax.axis_index("z").astype(jnp.uint32) + 4 * lax.axis_index("c").astype(jnp.uint32)

    w_all = lax.all_gather(w_up.T, "x", axis=0, tiled=False)

    near = jnp.broadcast_to(tokens[None], (16, rows, feats))
    near = lax.all_to_all(near, ("z", "yl"), split_axis=0, concat_axis=0).reshape(8, pair, feats)
    cot = along_z(within_z(act_grad, False), -1)
    near, cot = lax.optimization_barrier((near, cot))
    near = jnp.stack([cut(near, first, 4), cut(near, first + 4, 4)])
    near, cot, w_all = lax.optimization_barrier((near, cot, w_all))
    w_all = w_all.reshape(NX * cols, feats)

    sent = swap_cores(dot(near[1], w_all, ((1,), (1,))).astype(BF))
    partial_value = (dot(near[0], w_all, ((1,), (1,))) + sent.astype(jnp.float32)).astype(BF)
    partial_value = partial_value.reshape(4, pair, NX * cols)
    partial_value, cot = lax.optimization_barrier((partial_value, cot))
    parts = lax.all_to_all(partial_value, "yh", split_axis=0, concat_axis=0)
    hidden = jnp.sum(parts.astype(jnp.float32), axis=0)

    cot = in_order(shift_blocks(cot.reshape(NX, pair, cols), here), here)
    cot = cot.transpose(1, 0, 2).reshape(pair, NX * cols)

    activated, pullback = jax.vjp(gelu_tanh, hidden)
    hidden_grad = pullback(cot.astype(jnp.float32))[0].astype(BF)
    activated = activated.astype(BF)

    grad_own = jnp.broadcast_to(hidden_grad[None], (4, pair, NX * cols))
    grad_own = lax.all_to_all(grad_own, "yh", split_axis=0, concat_axis=0).reshape(4 * pair, NX * cols)
    activated = within_z(along_z(activated, 1), True)
    grad_own, activated = lax.optimization_barrier((grad_own, activated))
    grad_other = swap_cores(grad_own)

    ig_own = dot(grad_own, w_all, ((1,), (0,))).astype(BF)
    ig_own, grad_other = lax.optimization_barrier((ig_own, grad_other))
    ig_other = dot(grad_other, w_all, ((1,), (0,))).astype(BF)
    ig = cut(jnp.stack([ig_own, ig_other]).reshape(8, pair, feats), 16 - first, 8)
    ig, grad_own = lax.optimization_barrier((ig.reshape(16, rows, feats), grad_own))
    ig = lax.all_to_all(ig, ("z", "yl"), split_axis=0, concat_axis=0)

    far = lax.all_gather(near, "x", axis=0, tiled=False)
    far, grad_own, activated = lax.optimization_barrier((far, grad_own, activated))
    both = jnp.concatenate([grad_own, activated], axis=0)
    both = shift_blocks(both.reshape(5 * pair, NX, cols).transpose(1, 0, 2), here)
    far_own = in_order([part[: 4 * pair] for part in both], here)
    far_other = swap_cores(far_own)
    far_grad = jnp.stack([far_own, far_other], axis=1)
    weight_grad = dot(far.reshape(-1, feats), far_grad.reshape(-1, cols), ((0,), (0,))).astype(BF)
    out = in_order([part[4 * pair :] for part in both], here).reshape(NX * pair, cols)
    ig, weight_grad, out = lax.optimization_barrier((ig, weight_grad, out))
    input_grad = jnp.sum(ig.astype(jnp.float32), axis=0).astype(BF)
    return out, input_grad, weight_grad


def solution(mesh):
    fine = Mesh(mesh.devices.reshape(NX, 2, 8, 4, 2), AXES)
    in_specs = (P(("z", "x", "yl"), ("yh", "c")), P(("yh", "c"), ("x", "yl", "z")), P("z", ("x", "yl", "yh", "c")))
    out_specs = (in_specs[2], in_specs[0], in_specs[1])
    return jax.shard_map(body, mesh=fine, in_specs=in_specs, out_specs=out_specs, check_vma=False)
```

```python
import jax
import jax.numpy as jnp
from jax import lax
from jax.sharding import Mesh
from jax.sharding import PartitionSpec as P

AXES = ("x", "yl", "z", "yh", "c")
NX = 4
BF = jnp.bfloat16


def gelu_tanh(values):
    return jax.nn.gelu(values, approximate=True)


def along_x(value, shift):
    return lax.ppermute(value, "x", [(i, (i + shift) % NX) for i in range(NX)])


def swap_cores(value):
    return lax.ppermute(value, "c", [(0, 1), (1, 0)])


def turn(core, high):
    return 4 * core + high


def along_z(value, sign):
    pairs = []
    for z in range(8):
        for g in range(8):
            pairs.append((z * 8 + g, (z + sign * turn(g % 2, g // 2)) % 8 * 8 + g))
    return lax.ppermute(value, ("z", "yh", "c"), pairs)


def within_z(value, home):
    pairs = []
    for z in range(8):
        for g in range(8):
            pair = (z * 8 + g, z * 8 + (z - turn(g % 2, g // 2)) % 8)
            pairs.append(pair if home else pair[::-1])
    return lax.ppermute(value, ("z", "yh", "c"), pairs)


def shift_blocks(blocks, here):
    parts = []
    for r in range(NX):
        block = lax.dynamic_index_in_dim(blocks, (here + r) & (NX - 1), 0, keepdims=False)
        parts.append(along_x(block, r) if r else block)
    return parts


def in_order(parts, here, out=None):
    out = jnp.zeros((NX,) + parts[0].shape, BF) if out is None else out
    for r in range(NX):
        out = lax.dynamic_update_index_in_dim(out, parts[r], (here + (NX - r)) & (NX - 1), 0)
    return out


def cut(blocks, start, count):
    n, m = blocks.shape[1:]
    twice = jnp.concatenate([blocks, blocks], axis=0).reshape(16 * n, m)
    return lax.dynamic_slice_in_dim(twice, (start & 7) * n, count * n, 0)


def dot(a, b, contract):
    return lax.dot_general(a, b, (contract, ((), ())), preferred_element_type=jnp.float32)


def body(tokens, w_up, act_grad):
    rows, feats = tokens.shape
    cols = w_up.shape[1]
    pair = 2 * rows
    here = lax.axis_index("x").astype(jnp.uint32)
    first = lax.axis_index("z").astype(jnp.uint32) + 4 * lax.axis_index("c").astype(jnp.uint32)

    w_all = lax.all_gather(w_up.T, "x", axis=0, tiled=False)

    near = jnp.broadcast_to(tokens[None], (16, rows, feats))
    near = lax.all_to_all(near, ("z", "yl"), split_axis=0, concat_axis=0).reshape(8, pair, feats)
    cot = along_z(within_z(act_grad, False), -1)
    near, cot = lax.optimization_barrier((near, cot))
    near = jnp.stack([cut(near, first, 4), cut(near, first + 4, 4)])
    near, cot, w_all = lax.optimization_barrier((near, cot, w_all))
    w_all = w_all.reshape(NX * cols, feats)

    sent = swap_cores(dot(near[1], w_all, ((1,), (1,))).astype(BF))
    partial_value = (dot(near[0], w_all, ((1,), (1,))) + sent.astype(jnp.float32)).astype(BF)
    partial_value = partial_value.reshape(4, pair, NX * cols)
    partial_value, cot = lax.optimization_barrier((partial_value, cot))
    parts = lax.all_to_all(partial_value, "yh", split_axis=0, concat_axis=0)
    hidden = jnp.sum(parts.astype(jnp.float32), axis=0)

    cot = in_order(shift_blocks(cot.reshape(NX, pair, cols), here), here)
    cot = cot.transpose(1, 0, 2).reshape(pair, NX * cols)

    activated, pullback = jax.vjp(gelu_tanh, hidden)
    hidden_grad = pullback(cot.astype(jnp.float32))[0].astype(BF)
    activated = activated.astype(BF)

    grad_own = lax.all_gather(hidden_grad, "yh", axis=0, tiled=True)
    grad_own, activated = lax.optimization_barrier((grad_own, along_z(activated, 1)))
    grad_other = swap_cores(grad_own)
    activated = within_z(activated, True)

    ig_own = dot(grad_own, w_all, ((1,), (0,))).astype(BF)
    ig_own, grad_other = lax.optimization_barrier((ig_own, grad_other))
    ig_other = dot(grad_other, w_all, ((1,), (0,))).astype(BF)
    ig = cut(jnp.stack([ig_own, ig_other]).reshape(8, pair, feats), 16 - first, 8)
    ig, grad_own = lax.optimization_barrier((ig.reshape(16, rows, feats), grad_own))
    ig = lax.all_to_all(ig, ("z", "yl"), split_axis=0, concat_axis=0)

    far = lax.all_gather(near, "x", axis=0, tiled=False)
    far, grad_own, activated = lax.optimization_barrier((far, grad_own, activated))
    both = jnp.concatenate([grad_own, activated], axis=0)
    both = shift_blocks(both.reshape(5 * pair, NX, cols).transpose(1, 0, 2), here)
    far_own = in_order([part[: 4 * pair] for part in both], here)
    far_other = swap_cores(far_own)
    far_grad = jnp.stack([far_own, far_other], axis=1)
    weight_grad = dot(far.reshape(-1, feats), far_grad.reshape(-1, cols), ((0,), (0,))).astype(BF)
    out = in_order([part[4 * pair :] for part in both], here).reshape(NX * pair, cols)
    ig, weight_grad, out = lax.optimization_barrier((ig, weight_grad, out))
    input_grad = jnp.sum(ig.astype(jnp.float32), axis=0).astype(BF)
    return out, input_grad, weight_grad


def solution(mesh):
    fine = Mesh(mesh.devices.reshape(NX, 2, 8, 4, 2), AXES)
    in_specs = (P(("z", "x", "yl"), ("yh", "c")), P(("yh", "c"), ("x", "yl", "z")), P("z", ("x", "yl", "yh", "c")))
    out_specs = (in_specs[2], in_specs[0], in_specs[1])
    return jax.shard_map(body, mesh=fine, in_specs=in_specs, out_specs=out_specs, check_vma=False)
```

```python
import jax
import jax.numpy as jnp
from jax import lax
from jax.sharding import Mesh
from jax.sharding import PartitionSpec as P

AXES = ("x", "yl", "z", "yh", "c")
NX = 4
BF = jnp.bfloat16


def gelu_tanh(values):
    return jax.nn.gelu(values, approximate=True)


def along_x(value, shift):
    return lax.ppermute(value, "x", [(i, (i + shift) % NX) for i in range(NX)])


def swap_cores(value):
    return lax.ppermute(value, "c", [(0, 1), (1, 0)])


def turn(core, high):
    return 4 * core + high


def along_z(value, sign):
    pairs = []
    for z in range(8):
        for g in range(8):
            pairs.append((z * 8 + g, (z + sign * turn(g % 2, g // 2)) % 8 * 8 + g))
    return lax.ppermute(value, ("z", "yh", "c"), pairs)


def within_z(value, home):
    pairs = []
    for z in range(8):
        for g in range(8):
            pair = (z * 8 + g, z * 8 + (z - turn(g % 2, g // 2)) % 8)
            pairs.append(pair if home else pair[::-1])
    return lax.ppermute(value, ("z", "yh", "c"), pairs)


def shift_blocks(blocks, here):
    parts = []
    for r in range(NX):
        block = lax.dynamic_index_in_dim(blocks, (here + r) & (NX - 1), 0, keepdims=False)
        parts.append(along_x(block, r) if r else block)
    return parts


def in_order(parts, here, out=None):
    out = jnp.zeros((NX,) + parts[0].shape, BF) if out is None else out
    for r in range(NX):
        out = lax.dynamic_update_index_in_dim(out, parts[r], (here + (NX - r)) & (NX - 1), 0)
    return out


def cut(blocks, start, count):
    n, m = blocks.shape[1:]
    twice = jnp.concatenate([blocks, blocks], axis=0).reshape(16 * n, m)
    return lax.dynamic_slice_in_dim(twice, (start & 7) * n, count * n, 0)


def dot(a, b, contract):
    return lax.dot_general(a, b, (contract, ((), ())), preferred_element_type=jnp.float32)


def body(tokens, w_up, act_grad):
    rows, feats = tokens.shape
    cols = w_up.shape[1]
    pair = 2 * rows
    here = lax.axis_index("x").astype(jnp.uint32)
    first = lax.axis_index("z").astype(jnp.uint32) + 4 * lax.axis_index("c").astype(jnp.uint32)

    w_all = lax.all_gather(w_up.T, "x", axis=0, tiled=False)

    near = jnp.broadcast_to(tokens[None], (16, rows, feats))
    near = lax.all_to_all(near, ("z", "yl"), split_axis=0, concat_axis=0).reshape(8, pair, feats)
    cot = along_z(within_z(act_grad, False), -1)
    near, cot = lax.optimization_barrier((near, cot))
    near = jnp.stack([cut(near, first, 4), cut(near, first + 4, 4)])
    near, cot, w_all = lax.optimization_barrier((near, cot, w_all))
    w_all = w_all.reshape(NX * cols, feats)

    sent = swap_cores(dot(near[1], w_all, ((1,), (1,))).astype(BF))
    partial_value = (dot(near[0], w_all, ((1,), (1,))) + sent.astype(jnp.float32)).astype(BF)
    partial_value = partial_value.reshape(4, pair, NX * cols)
    partial_value, cot = lax.optimization_barrier((partial_value, cot))
    parts = lax.all_to_all(partial_value, "yh", split_axis=0, concat_axis=0)
    hidden = jnp.sum(parts.astype(jnp.float32), axis=0)

    cot = in_order(shift_blocks(cot.reshape(NX, pair, cols), here), here)
    cot = cot.transpose(1, 0, 2).reshape(pair, NX * cols)

    activated, pullback = jax.vjp(gelu_tanh, hidden)
    hidden_grad = pullback(cot.astype(jnp.float32))[0].astype(BF)
    activated = activated.astype(BF)

    grad_own = lax.all_gather(hidden_grad, "yh", axis=0, tiled=True)
    grad_own, activated = lax.optimization_barrier((grad_own, along_z(activated, 1)))
    grad_other = swap_cores(grad_own)
    activated = within_z(activated, True)

    ig_own = dot(grad_own, w_all, ((1,), (0,))).astype(BF)
    ig_own, grad_other = lax.optimization_barrier((ig_own, grad_other))
    ig_other = dot(grad_other, w_all, ((1,), (0,))).astype(BF)
    ig = cut(jnp.stack([ig_own, ig_other]).reshape(8, pair, feats), 16 - first, 8)
    ig, grad_own = lax.optimization_barrier((ig.reshape(16, rows, feats), grad_own))
    ig = lax.all_to_all(ig, ("z", "yl"), split_axis=0, concat_axis=0)

    far = lax.all_gather(near, "x", axis=0, tiled=False)
    far, grad_own, activated = lax.optimization_barrier((far, grad_own, activated))
    blocks = shift_blocks(grad_own.reshape(4 * pair, NX, cols).transpose(1, 0, 2), here)
    moved = shift_blocks(activated.reshape(pair, NX, cols).transpose(1, 0, 2), here)
    far_own = in_order(blocks, here)
    far_own, moved[1] = lax.optimization_barrier((far_own, moved[1]))
    far_other = swap_cores(far_own)
    far_grad = jnp.stack([far_own, far_other], axis=1)
    weight_grad = dot(far.reshape(-1, feats), far_grad.reshape(-1, cols), ((0,), (0,))).astype(BF)
    out = in_order(moved, here).reshape(NX * pair, cols)
    ig, weight_grad, out = lax.optimization_barrier((ig, weight_grad, out))
    input_grad = jnp.sum(ig.astype(jnp.float32), axis=0).astype(BF)
    return out, input_grad, weight_grad


def solution(mesh):
    fine = Mesh(mesh.devices.reshape(NX, 2, 8, 4, 2), AXES)
    in_specs = (P(("z", "x", "yl"), ("yh", "c")), P(("yh", "c"), ("x", "yl", "z")), P("z", ("x", "yl", "yh", "c")))
    out_specs = (in_specs[2], in_specs[0], in_specs[1])
    return jax.shard_map(body, mesh=fine, in_specs=in_specs, out_specs=out_specs, check_vma=False)
```

```python
import jax
import jax.numpy as jnp
from jax import lax
from jax.sharding import Mesh
from jax.sharding import PartitionSpec as P

AXES = ("x", "yl", "z", "yh", "c")
NX = 4
BF = jnp.bfloat16


def gelu_tanh(values):
    return jax.nn.gelu(values, approximate=True)


def along_x(value, shift):
    return lax.ppermute(value, "x", [(i, (i + shift) % NX) for i in range(NX)])


def swap_cores(value):
    return lax.ppermute(value, "c", [(0, 1), (1, 0)])


def turn(core, high):
    return 4 * core + high


def along_z(value, sign):
    pairs = []
    for z in range(8):
        for g in range(8):
            pairs.append((z * 8 + g, (z + sign * turn(g % 2, g // 2)) % 8 * 8 + g))
    return lax.ppermute(value, ("z", "yh", "c"), pairs)


def within_z(value, home):
    pairs = []
    for z in range(8):
        for g in range(8):
            pair = (z * 8 + g, z * 8 + (z - turn(g % 2, g // 2)) % 8)
            pairs.append(pair if home else pair[::-1])
    return lax.ppermute(value, ("z", "yh", "c"), pairs)


def shift_blocks(blocks, here):
    parts = []
    for r in range(NX):
        block = lax.dynamic_index_in_dim(blocks, (here + r) & (NX - 1), 0, keepdims=False)
        parts.append(along_x(block, r) if r else block)
    return parts


def in_order(parts, here, out=None):
    out = jnp.zeros((NX,) + parts[0].shape, BF) if out is None else out
    for r in range(NX):
        out = lax.dynamic_update_index_in_dim(out, parts[r], (here + (NX - r)) & (NX - 1), 0)
    return out


def cut(blocks, start, count):
    n, m = blocks.shape[1:]
    twice = jnp.concatenate([blocks, blocks], axis=0).reshape(16 * n, m)
    return lax.dynamic_slice_in_dim(twice, (start & 7) * n, count * n, 0)


def dot(a, b, contract):
    return lax.dot_general(a, b, (contract, ((), ())), preferred_element_type=jnp.float32)


def body(tokens, w_up, act_grad):
    rows, feats = tokens.shape
    cols = w_up.shape[1]
    pair = 2 * rows
    here = lax.axis_index("x").astype(jnp.uint32)
    first = lax.axis_index("z").astype(jnp.uint32) + 4 * lax.axis_index("c").astype(jnp.uint32)

    w_all = lax.all_gather(w_up.T, "x", axis=0, tiled=False)

    near = jnp.broadcast_to(tokens[None], (16, rows, feats))
    near = lax.all_to_all(near, ("z", "yl"), split_axis=0, concat_axis=0).reshape(8, pair, feats)
    cot = along_z(within_z(act_grad, False), -1)
    near, cot = lax.optimization_barrier((near, cot))
    near = jnp.stack([cut(near, first, 4), cut(near, first + 4, 4)])
    near, cot, w_all = lax.optimization_barrier((near, cot, w_all))
    w_all = w_all.reshape(NX * cols, feats)

    sent = swap_cores(dot(near[1], w_all, ((1,), (1,))).astype(BF))
    partial_value = (dot(near[0], w_all, ((1,), (1,))) + sent.astype(jnp.float32)).astype(BF)
    partial_value = partial_value.reshape(4, pair, NX * cols)
    partial_value, cot = lax.optimization_barrier((partial_value, cot))
    parts = lax.all_to_all(partial_value, "yh", split_axis=0, concat_axis=0)
    hidden = jnp.sum(parts.astype(jnp.float32), axis=0)

    cot = in_order(shift_blocks(cot.reshape(NX, pair, cols), here), here)
    cot = cot.transpose(1, 0, 2).reshape(pair, NX * cols)

    activated, pullback = jax.vjp(gelu_tanh, hidden)
    hidden_grad = pullback(cot.astype(jnp.float32))[0].astype(BF)
    activated = activated.astype(BF)

    grad_own = lax.all_gather(hidden_grad, "yh", axis=0, tiled=True)
    grad_own, activated = lax.optimization_barrier((grad_own, along_z(activated, 1)))
    grad_other = swap_cores(grad_own)
    activated = within_z(activated, True)

    ig_own = dot(grad_own, w_all, ((1,), (0,))).astype(BF)
    ig_own, grad_other = lax.optimization_barrier((ig_own, grad_other))
    ig_other = dot(grad_other, w_all, ((1,), (0,))).astype(BF)
    ig = cut(jnp.stack([ig_own, ig_other]).reshape(8, pair, feats), 16 - first, 8)
    ig, grad_own = lax.optimization_barrier((ig.reshape(16, rows, feats), grad_own))
    ig = lax.all_to_all(ig, ("z", "yl"), split_axis=0, concat_axis=0)

    far = lax.all_gather(near, "x", axis=0, tiled=False)
    far, grad_own, activated = lax.optimization_barrier((far, grad_own, activated))
    blocks = shift_blocks(grad_own.reshape(4 * pair, NX, cols).transpose(1, 0, 2), here)
    moved = shift_blocks(activated.reshape(pair, NX, cols).transpose(1, 0, 2), here)
    far_own = in_order(blocks, here)
    far_own, *moved = lax.optimization_barrier((far_own, *moved))
    far_other = swap_cores(far_own)
    far_grad = jnp.stack([far_own, far_other], axis=1)
    weight_grad = dot(far.reshape(-1, feats), far_grad.reshape(-1, cols), ((0,), (0,))).astype(BF)
    out = in_order(moved, here).reshape(NX * pair, cols)
    ig, weight_grad, out = lax.optimization_barrier((ig, weight_grad, out))
    input_grad = jnp.sum(ig.astype(jnp.float32), axis=0).astype(BF)
    return out, input_grad, weight_grad


def solution(mesh):
    fine = Mesh(mesh.devices.reshape(NX, 2, 8, 4, 2), AXES)
    in_specs = (P(("z", "x", "yl"), ("yh", "c")), P(("yh", "c"), ("x", "yl", "z")), P("z", ("x", "yl", "yh", "c")))
    out_specs = (in_specs[2], in_specs[0], in_specs[1])
    return jax.shard_map(body, mesh=fine, in_specs=in_specs, out_specs=out_specs, check_vma=False)
```
